128 devices in a mesh: dom: 128 (over z, x, y, core).
Axes of the slice: x: 4, y: 4, z: 4, core: 2. Of those that a mesh axis runs over, the one named last changes fastest.
Arguments:
- node_latent: bfloat16 [65536, 512], P('dom'), may hold values from -6 to 6
- edge_latent: bfloat16 [262144, 512], P('dom'), may hold values from -6 to 6
- sender_index: int32 [262144], P('dom'), may hold values from 0 to 1535, as said below
- receiver_index: int32 [262144], P('dom'), may hold values from 0 to 511
- send_rows: int32 [128, 128, 8], P('dom'), may hold values from 0 to 511
- node_count: int32 [128], P('dom'), may hold values from 256 to 512, as said below
- edge_proj_in: bfloat16 [1, 1536, 512], replicated, may hold values from -0.15625 to 0.15625
- edge_bias_in: float32 [1, 512], replicated, may hold values from -3 to 3
- edge_proj_out: bfloat16 [1, 512, 512], replicated, may hold values from -0.25 to 0.25
- edge_bias_out: float32 [1, 512], replicated, may hold values from -3 to 3
- edge_gain: float32 [1, 512], replicated, may hold values from 0.1 to 1.9
- node_proj_in: bfloat16 [1, 1024, 512], replicated, may hold values from -0.1875 to 0.1875
- node_bias_in: float32 [1, 512], replicated, may hold values from -3 to 3
- node_proj_out: bfloat16 [1, 512, 512], replicated, may hold values from -0.25 to 0.25
- node_bias_out: float32 [1, 512], replicated, may hold values from -3 to 3
- node_gain: float32 [1, 512], replicated, may hold values from 0.1 to 1.9
- node_cot: float32 [65536, 512], P('dom'), may hold values from -6 to 6
- edge_cot: float32 [262144, 512], P('dom'), may hold values from -6 to 6
Outputs:
- node_out: bfloat16 [65536, 512], P('dom')
- edge_out: bfloat16 [262144, 512], P('dom')
- node_grad: float32 [65536, 512], P('dom')
- edge_grad: float32 [262144, 512], P('dom')
- edge_in_grad: float32 [1, 1536, 512], P(None, 'dom')
- edge_out_grad: float32 [1, 512, 512], P(None, 'dom')
- node_in_grad: float32 [1, 1024, 512], P(None, 'dom')
- node_out_grad: float32 [1, 512, 512], P(None, 'dom')
The draws below stay inside these ranges and needn't reach their ends.
Inputs may be any that keep to these rules, and one draw needn't show every extreme that they name: `sender_index`: values below 512 name a node of the edge's own partition; 512 + p * 8 + k names entry k of the list that partition p sends to the edge's partition d. Most senders are local; remote ones come from partitions p = (d + t) mod 128 with t in -4 .. 4 or t = 64, never p = d. `receiver_index`: local node numbers of the edge's own partition; receivers at or above the partition's node count are padding. send_rows[p, q] lists local nodes of partition p; entries may repeat. `node_count`: some partition holds exactly 512 real nodes and some exactly 256.
All inputs are finite; a program needn't handle non-finite values.
Results may differ from the reference program's by a relative error of at most 0.017.
Values may be sent and summed in bfloat16 or wider, within the bound.
A program may use at most 192 MiB of HBM per device.

```python
import jax
import jax.numpy as jnp
from jax import lax

L = 512
LAYERS = 1
NODE_DEV = 512
EDGE_DEV = 2048
HB = 8
NODES = 65536
EDGES = 262144
N_DOM = 128


def draw_node_count(key, part):
    key = jax.random.fold_in(key, 11)
    first_key, second_key, third_key = jax.random.split(key, 3)
    parts_total = NODES // NODE_DEV
    counts = jax.random.randint(first_key, (parts_total,), NODE_DEV // 2, NODE_DEV + 1)
    top_pos = jax.random.randint(second_key, (), 0, parts_total)
    low_pos = (top_pos + 1 + jax.random.randint(third_key, (), 0, parts_total - 1)) % parts_total
    counts = counts.at[top_pos].set(NODE_DEV).at[low_pos].set(NODE_DEV // 2)
    return counts.astype(jnp.int32)


def draw_sender_index(key, part):
    key = jax.random.fold_in(key, 5)
    local_key, pick_key, offset_key, slot_key = jax.random.split(key, 4)
    parts_total = EDGES // EDGE_DEV
    edge_ids = jnp.arange(EDGES, dtype=jnp.int32)
    owner = edge_ids // EDGE_DEV
    position = edge_ids % EDGE_DEV
    local_value = jax.random.randint(local_key, (EDGES,), 0, NODE_DEV)
    local_value = jnp.where(position == 3, 0, local_value)
    pick = jax.random.randint(pick_key, (EDGES,), 0, 100)
    near_table = jnp.array([1, -1, 2, -2, 3, -3, 4, -4], dtype=jnp.int32)
    near_pick = jax.random.randint(offset_key, (EDGES,), 0, 8)
    offset = jnp.where(pick < 2, parts_total // 2, near_table[near_pick])
    offset = jnp.where(position == 0, parts_total // 2, offset)
    offset = jnp.where(position == 1, 1, offset)
    offset = jnp.where(position == 2, -1, offset)
    slot = jax.random.randint(slot_key, (EDGES,), 0, HB)
    slot = jnp.where(position == 2, HB - 1, slot)
    peer = (owner + offset + parts_total) % parts_total
    remote = (pick < 14) & (position > 3) | (position < 3)
    value = jnp.where(remote, NODE_DEV + peer * HB + slot, local_value)
    return value.astype(jnp.int32)


def set_ends(result, key, low, high):
    shape = result.shape
    spot = [jax.random.randint(jax.random.fold_in(key, axis), (), 0, shape[axis]) for axis in range(len(shape))]
    result = result.at[tuple(spot)].set(low)
    longest = shape.index(max(shape))
    spot[longest] = (spot[longest] + 1) % shape[longest]
    return result.at[tuple(spot)].set(high)


def levels(key, shape, shards, least, largest):
    loudness = 1.0
    for dim, shards_of in shards:
        steps = jax.random.uniform(jax.random.fold_in(jax.random.fold_in(key, 6), dim), (shards_of,), jnp.float32, least / len(shards), largest / len(shards))
        loudness = loudness * jnp.repeat(jnp.exp(steps), shape[dim] // shards_of).reshape((-1,) + (1,) * (len(shape) - 1 - dim))
    return loudness


def bell_draw(rng, dims, scale, most, shards=(), kind=jnp.bfloat16):
    drawn = jax.random.normal(rng, dims, jnp.float32) * scale
    if len(shards) > 0:
        drawn = levels(rng, dims, shards, -0.22, 0.18) * drawn
    return jnp.clip(drawn, min=-most, max=most).astype(kind)


def setup_inputs(seed: int = 0) -> dict:
    key_of = jax.random.split(jax.random.key(seed), 19)
    return {
        "node_latent": bell_draw(key_of[0], (NODES, L), 1.0, 6.0, ((0, 128),)),
        "edge_latent": bell_draw(key_of[1], (EDGES, L), 1.0, 6.0, ((0, 128),)),
        "sender_index": draw_sender_index(jax.random.fold_in(key_of[18], 71), 0),
        "receiver_index": set_ends(jax.random.randint(key_of[3], (EDGES,), 0, NODE_DEV), jax.random.fold_in(key_of[3], 1), 0, NODE_DEV - 1).astype(jnp.int32),
        "send_rows": set_ends(jax.random.randint(key_of[4], (N_DOM, N_DOM, HB), 0, NODE_DEV), jax.random.fold_in(key_of[4], 1), 0, NODE_DEV - 1).astype(jnp.int32),
        "node_count": draw_node_count(jax.random.fold_in(key_of[18], 71), 0),
        "edge_proj_in": bell_draw(key_of[6], (LAYERS, 3 * L, L), (3 * L) ** -0.5, 0.15625),
        "edge_bias_in": bell_draw(key_of[7], (LAYERS, L), 0.5, 3.0, (), jnp.float32),
        "edge_proj_out": bell_draw(key_of[8], (LAYERS, L, L), L ** -0.5, 0.25),
        "edge_bias_out": bell_draw(key_of[9], (LAYERS, L), 0.5, 3.0, (), jnp.float32),
        "edge_gain": jnp.clip(1.0 + 0.18 * jax.random.normal(key_of[10], (LAYERS, L), jnp.float32), 0.1, 1.9),
        "node_proj_in": bell_draw(key_of[11], (LAYERS, 2 * L, L), (2 * L) ** -0.5, 0.1875),
        "node_bias_in": bell_draw(key_of[12], (LAYERS, L), 0.5, 3.0, (), jnp.float32),
        "node_proj_out": bell_draw(key_of[13], (LAYERS, L, L), L ** -0.5, 0.25),
        "node_bias_out": bell_draw(key_of[14], (LAYERS, L), 0.5, 3.0, (), jnp.float32),
        "node_gain": jnp.clip(1.0 + 0.18 * jax.random.normal(key_of[15], (LAYERS, L), jnp.float32), 0.1, 1.9),
        "node_cot": bell_draw(key_of[16], (NODES, L), 1.0, 6.0, ((0, 128),), jnp.float32),
        "edge_cot": bell_draw(key_of[17], (EDGES, L), 1.0, 6.0, ((0, 128),), jnp.float32),
    }


EPS = 1e-05

def mlp_forward(features, proj_in, bias_in, proj_out, bias_out, gain_vec):
    pre_act = jnp.dot(features, proj_in, preferred_element_type=jnp.float32) + bias_in
    hidden_act = (pre_act * jax.nn.sigmoid(pre_act)).astype(jnp.bfloat16)
    raw_out = jnp.dot(hidden_act, proj_out, preferred_element_type=jnp.float32) + bias_out
    centered = raw_out - lax.optimization_barrier(jnp.mean(raw_out, axis=-1, keepdims=True))
    inv_scale = lax.rsqrt(lax.optimization_barrier(jnp.mean(centered * centered, axis=-1, keepdims=True)) + EPS)
    normed = centered * inv_scale
    return (normed * gain_vec, (pre_act, hidden_act, normed, inv_scale))

def mlp_backward(saved, proj_in, proj_out, gain_vec, cotangent):
    pre_act, hidden_act, normed, inv_scale = saved
    scaled_cot = cotangent * gain_vec
    grad_raw = inv_scale * (scaled_cot - lax.optimization_barrier(jnp.mean(scaled_cot, axis=-1, keepdims=True)) - normed * lax.optimization_barrier(jnp.mean(scaled_cot * normed, axis=-1, keepdims=True)))
    grad_out = grad_raw.astype(jnp.bfloat16)
    contract = (((1,), (1,)), ((), ()))
    grad_hidden = lax.dot_general(grad_out, proj_out, contract, preferred_element_type=jnp.float32)
    gate_sig = jax.nn.sigmoid(pre_act)
    grad_pre = (grad_hidden * gate_sig * (1.0 + pre_act * (1.0 - gate_sig))).astype(jnp.bfloat16)
    grad_feat = lax.dot_general(grad_pre, proj_in, contract, preferred_element_type=jnp.float32)
    return (grad_feat, grad_out, grad_pre)

def weight_term(left, right):
    return lax.dot_general(left, right, (((0,), (0,)), ((), ())), preferred_element_type=jnp.float32)

def reference(node_latent, edge_latent, sender_index, receiver_index, send_rows, node_count, edge_proj_in, edge_bias_in, edge_proj_out, edge_bias_out, edge_gain, node_proj_in, node_bias_in, node_proj_out, node_bias_out, node_gain, node_cot, edge_cot):
    latent_width = node_latent.shape[1]
    edge_owner = jnp.arange(EDGES, dtype=jnp.int32) // EDGE_DEV
    slot_index = jnp.maximum(sender_index - NODE_DEV, 0).astype(jnp.int32)
    peer_index = slot_index // HB
    slot_pos = slot_index % HB
    remote_row = send_rows[peer_index, edge_owner, slot_pos]
    sender = jnp.where(sender_index < NODE_DEV, edge_owner * NODE_DEV + sender_index, peer_index * NODE_DEV + remote_row).astype(jnp.int32)
    receiver = (edge_owner * NODE_DEV + receiver_index).astype(jnp.int32)
    node_ids = jnp.arange(NODES, dtype=jnp.int32)
    node_valid = (node_ids % NODE_DEV < node_count[node_ids // NODE_DEV]).astype(jnp.float32)[:, None]
    edge_live = (receiver_index < node_count[edge_owner]).astype(jnp.float32)[:, None]
    current_nodes, current_edges = (node_latent, edge_latent)
    caches = []
    for layer_index in range(LAYERS):
        features = jnp.concatenate([current_edges, jnp.take(current_nodes, sender, axis=0), jnp.take(current_nodes, receiver, axis=0)], axis=1)
        edge_update, edge_saved = mlp_forward(features, edge_proj_in[layer_index], edge_bias_in[layer_index], edge_proj_out[layer_index], edge_bias_out[layer_index], edge_gain[layer_index])
        new_edges = (current_edges.astype(jnp.float32) + edge_update).astype(jnp.bfloat16)
        summed = jnp.zeros((NODES, latent_width), jnp.float32).at[receiver].add(edge_live * new_edges.astype(jnp.float32))
        node_features = jnp.concatenate([current_nodes, summed.astype(jnp.bfloat16)], axis=1)
        node_update, node_saved = mlp_forward(node_features, node_proj_in[layer_index], node_bias_in[layer_index], node_proj_out[layer_index], node_bias_out[layer_index], node_gain[layer_index])
        new_nodes = (current_nodes.astype(jnp.float32) + node_valid * node_update).astype(jnp.bfloat16)
        caches.append((features, edge_saved, node_features, node_saved))
        current_nodes, current_edges = (new_nodes, new_edges)
    node_out, edge_out = (current_nodes, current_edges)
    edge_scale = EDGES ** (-0.5)
    node_scale = NODES ** (-0.5)
    grad_nodes, grad_edges = (node_cot, edge_cot)
    grads_edge_in = [None] * LAYERS
    grads_edge_out = [None] * LAYERS
    grads_node_in = [None] * LAYERS
    grads_node_out = [None] * LAYERS
    for layer_index in reversed(range(LAYERS)):
        features, edge_saved, node_features, node_saved = caches[layer_index]
        node_feat_grad, node_grad_out, node_grad_pre = mlp_backward(node_saved, node_proj_in[layer_index], node_proj_out[layer_index], node_gain[layer_index], node_valid * grad_nodes)
        edge_total = grad_edges + edge_live * jnp.take(node_feat_grad[:, latent_width:], receiver, axis=0)
        edge_feat_grad, edge_grad_out, edge_grad_pre = mlp_backward(edge_saved, edge_proj_in[layer_index], edge_proj_out[layer_index], edge_gain[layer_index], edge_total)
        next_edges = edge_total + edge_feat_grad[:, :latent_width]
        next_nodes = grad_nodes + node_feat_grad[:, :latent_width]
        next_nodes = next_nodes.at[sender].add(edge_feat_grad[:, latent_width:2 * latent_width])
        next_nodes = next_nodes.at[receiver].add(edge_feat_grad[:, 2 * latent_width:])
        grads_edge_in[layer_index] = weight_term(features, edge_grad_pre) * edge_scale
        grads_edge_out[layer_index] = weight_term(edge_saved[1], edge_grad_out) * edge_scale
        grads_node_in[layer_index] = weight_term(node_features, node_grad_pre) * node_scale
        grads_node_out[layer_index] = weight_term(node_saved[1], node_grad_out) * node_scale
        grad_nodes, grad_edges = (next_nodes, next_edges)
    return (node_out, edge_out, grad_nodes, grad_edges, jnp.stack(grads_edge_in), jnp.stack(grads_edge_out), jnp.stack(grads_node_in), jnp.stack(grads_node_out))
```

```python
import functools

import jax
import jax.numpy as jnp
from jax import lax
from jax.experimental import pallas as pl
from jax.experimental.pallas import tpu as pltpu
from jax.sharding import PartitionSpec as P

EPS = 1e-05
MESH = pl.DeviceIdType.MESH
BF = jnp.bfloat16
F32 = jnp.float32
I32 = jnp.int32

L = 512
N = 512
E = 2048
HB = 8
SLOTS = 9
HALO = SLOTS * HB
HPAD = 128
TAB = N + HPAD
C = 256
CHUNKS = E // C
XW = L + TAB + N
VMEM_LIMIT = 56 * 1024 * 1024

NT = (((1,), (1,)), ((), ()))
TN = (((0,), (0,)), ((), ()))


def slot_shift(slot):
    return 64 if slot == 4 else slot - 4


def mm(a, b):
    return jnp.dot(a, b, preferred_element_type=F32)


def mm_nt(a, b):
    return lax.dot_general(a, b, NT, preferred_element_type=F32)


def mm_tn(a, b):
    return lax.dot_general(a, b, TN, preferred_element_type=F32)


def sigmoid(x):
    return 0.5 * jnp.tanh(0.5 * x) + 0.5


def table_index(sender, me, n_dom):
    far = sender - N
    peer = far // HB
    row = far - peer * HB
    turn = lax.rem(peer - me + (n_dom + 4), n_dom)
    slot = jnp.where(turn == 68, 4, turn)
    return jnp.where(sender < N, sender, N + slot * HB + row)


def greet(devices):
    barrier = pltpu.get_barrier_semaphore()
    for device in devices:
        pl.semaphore_signal(barrier, inc=1, device_id=(device,), device_id_type=MESH)
    pl.semaphore_wait(barrier, len(devices))


def halo_kernel(n_dom, h_ref, rows_ref, out_ref, wide, outgoing, incoming, send_sem, recv_sem):
    me = lax.axis_index("dom")
    targets = [lax.rem(me - slot_shift(s) + n_dom, n_dom) for s in range(SLOTS)]
    wide[...] = h_ref[...].astype(F32)
    barrier = pltpu.get_barrier_semaphore()
    for device in targets:
        pl.semaphore_signal(barrier, inc=1, device_id=(device,), device_id_type=MESH)
    for s in range(SLOTS):
        for k in range(HB):
            row = rows_ref[targets[s] * HB + k]
            outgoing[pl.ds(s * HB + k, 1), :] = wide[pl.ds(row, 1), :]
    pl.semaphore_wait(barrier, SLOTS)
    copies = []
    for s in range(SLOTS):
        copy = pltpu.make_async_remote_copy(
            src_ref=outgoing.at[pl.ds(s * HB, HB)],
            dst_ref=incoming.at[pl.ds(s * HB, HB)],
            send_sem=send_sem.at[s],
            recv_sem=recv_sem.at[s],
            device_id=(targets[s],),
            device_id_type=MESH,
        )
        copy.start()
        copies.append(copy)
    for copy in copies:
        copy.wait()
    out_ref[...] = jnp.concatenate(
        [incoming[...].astype(BF), jnp.zeros((HPAD - HALO, L), BF)], axis=0
    )


def fetch_halo(node_rows, slot_rows, n_dom):
    return pl.pallas_call(
        functools.partial(halo_kernel, n_dom),
        out_shape=jax.ShapeDtypeStruct((HPAD, L), BF),
        in_specs=[
            pl.BlockSpec(memory_space=pltpu.VMEM),
            pl.BlockSpec(memory_space=pltpu.SMEM),
        ],
        out_specs=pl.BlockSpec(memory_space=pltpu.VMEM),
        scratch_shapes=[
            pltpu.VMEM((N, L), F32),
            pltpu.VMEM((HALO, L), F32),
            pltpu.VMEM((HALO, L), F32),
            pltpu.SemaphoreType.DMA((SLOTS,)),
            pltpu.SemaphoreType.DMA((SLOTS,)),
        ],
        compiler_params=pltpu.CompilerParams(collective_id=0, has_side_effects=True),
        name="halo",
    )(node_rows, slot_rows)


def norm_forward(raw):
    centered = raw - jnp.mean(raw, axis=-1, keepdims=True)
    inv = lax.rsqrt(jnp.mean(centered * centered, axis=-1, keepdims=True) + EPS)
    return centered * inv, inv


def norm_backward(q, normed, inv):
    first = jnp.mean(q, axis=-1, keepdims=True)
    second = jnp.mean(q * normed, axis=-1, keepdims=True)
    return inv * (q - first - normed * second)


def act_slope(pre):
    gate = sigmoid(pre)
    return gate * (1.0 + pre * (1.0 - gate))


def rows_kernel(
    n_dom,
    snd_ref, rcv_ref, cnt_ref, h_hbm, halo_hbm, e_hbm, pin_hbm, b_in, pout_hbm, b_out, gain,
    npin_hbm, nb_in, npout_hbm, nb_out, ngain, ncot_hbm, ecot_hbm,
    nout_hbm, eout_hbm, egrad_hbm, dpre_hbm, draw_hbm, hid_hbm, gnode_hbm, npart_hbm,
    idx_v, x_v, rt_v, w_v, tab_v, pin_v, pout_v, npin_v, npout_v, ncot_v, cot_v,
    pre_v, hid_v, n_v, inv_v, enew_v, draw_v, dpre_v, nx_v, dy_v, nout_v, npart_v, gnode_v,
    in_sem, e_sem, cot_sem, eout_sem, hid_sem, draw_sem, dpre_sem, egrad_sem, out_sem,
):
    me = lax.axis_index("dom")

    def load(k, src, dst):
        return pltpu.make_async_copy(src, dst, in_sem.at[k])

    def rows(i):
        return pl.ds(pl.multiple_of(i * C, C), C)

    def e_load(i):
        return pltpu.make_async_copy(e_hbm.at[rows(i)], x_v.at[rows(i), pl.ds(0, L)], e_sem.at[i])

    def cot_load(i):
        return pltpu.make_async_copy(ecot_hbm.at[rows(i)], cot_v.at[rows(i)], cot_sem.at[i])

    def put(i, src, dst, sem):
        return pltpu.make_async_copy(src.at[rows(i)], dst.at[rows(i)], sem.at[i])

    loads = [
        load(0, h_hbm, tab_v.at[pl.ds(0, N)]),
        load(1, halo_hbm, tab_v.at[pl.ds(N, HPAD)]),
        load(2, pin_hbm, pin_v),
        load(3, pout_hbm, pout_v),
        load(4, npin_hbm, npin_v),
        load(5, npout_hbm, npout_v),
        load(6, ncot_hbm, ncot_v),
    ]
    for k in range(3):
        loads[k].start()
    for i in range(CHUNKS):
        e_load(i).start()
    for k in range(3, 7):
        loads[k].start()
    for i in range(CHUNKS):
        cot_load(i).start()

    idx_v[...] = table_index(snd_ref[...], me, n_dom)
    lane = lax.broadcasted_iota(I32, (128, 128), 1)
    high = lax.broadcasted_iota(I32, (N, 128), 0)

    for k in range(3):
        loads[k].wait()
    w_v[0:L, :] = pin_v[0:L, :]
    w_v[L : L + TAB, :] = mm(tab_v[...], pin_v[L : 2 * L, :]).astype(BF)
    w_v[L + TAB :, :] = (mm(tab_v[0:N, :], pin_v[2 * L :, :]) + b_in[...]).astype(BF)
    loads[3].wait()

    def forward(i, carry):
        e_load(i).wait()
        for b in range(C // 128):
            block = i * (C // 128) + b
            at = pl.ds(pl.multiple_of(block * 128, 128), 128)
            s_col = jnp.broadcast_to(idx_v[pl.ds(block, 1), :], (128, 128)).T
            r_row = rcv_ref[pl.ds(block, 1), :]
            r_col = jnp.broadcast_to(r_row, (128, 128)).T
            for m in range(TAB // 128):
                x_v[at, L + 128 * m : L + 128 * (m + 1)] = (s_col == lane + 128 * m).astype(F32).astype(BF)
            for m in range(N // 128):
                x_v[at, L + TAB + 128 * m : L + TAB + 128 * (m + 1)] = (
                    (r_col == lane + 128 * m).astype(F32).astype(BF)
                )
            rt_v[:, at] = (jnp.broadcast_to(r_row, (N, 128)) == high).astype(F32).astype(BF)
        pre = mm(x_v[rows(i), :], w_v[...])
        pre_v[rows(i), :] = pre
        hid = (pre * sigmoid(pre)).astype(BF)
        hid_v[rows(i), :] = hid
        raw = mm(hid, pout_v[...]) + b_out[...]
        normed, inv = norm_forward(raw)
        n_v[rows(i), :] = normed
        inv_v[rows(i), :] = inv
        enew_v[rows(i), :] = (x_v[rows(i), 0:L].astype(F32) + normed * gain[...]).astype(BF)
        put(i, enew_v, eout_hbm, eout_sem).start()
        put(i, hid_v, hid_hbm, hid_sem).start()
        return carry

    lax.fori_loop(0, CHUNKS, forward, 0)

    valid = (lax.broadcasted_iota(I32, (N, 1), 0) < cnt_ref[0]).astype(F32)
    nx_v[:, 0:L] = tab_v[0:N, :]
    nx_v[:, L:] = (mm(rt_v[...], enew_v[...]) * valid).astype(BF)
    for k in range(4, 7):
        loads[k].wait()
    pre = mm(nx_v[...], npin_v[...]) + nb_in[...]
    hid = (pre * sigmoid(pre)).astype(BF)
    normed, inv = norm_forward(mm(hid, npout_v[...]) + nb_out[...])
    nout_v[...] = (tab_v[0:N, :].astype(F32) + valid * (normed * ngain[...])).astype(BF)
    nout_copy = pltpu.make_async_copy(nout_v, nout_hbm, out_sem.at[0])
    nout_copy.start()
    draw = norm_backward(valid * ncot_v[...] * ngain[...], normed, inv).astype(BF)
    dpre = (mm_nt(draw, npout_v[...]) * act_slope(pre)).astype(BF)
    npart_v[...] = ncot_v[...] + mm_nt(dpre, npin_v[0:L, :])
    npart_copy = pltpu.make_async_copy(npart_v, npart_hbm, out_sem.at[1])
    npart_copy.start()
    dy_v[...] = mm_nt(dpre, npin_v[L:, :]).astype(BF)
    gnode_v[:, 0:64, :] = mm_tn(nx_v[...], dpre).astype(BF).reshape(16, 64, L)
    gnode_v[:, 64:96, :] = mm_tn(hid, draw).astype(BF).reshape(16, 32, L)
    gnode_copy = pltpu.make_async_copy(gnode_v, gnode_hbm, out_sem.at[2])
    gnode_copy.start()

    def backward(i, carry):
        cot_load(i).wait()
        total = cot_v[rows(i), :] + mm(x_v[rows(i), L + TAB :], dy_v[...])
        draw = norm_backward(total * gain[...], n_v[rows(i), :], inv_v[rows(i), :]).astype(BF)
        draw_v[rows(i), :] = draw
        put(i, draw_v, draw_hbm, draw_sem).start()
        dpre = (mm_nt(draw, pout_v[...]) * act_slope(pre_v[rows(i), :])).astype(BF)
        dpre_v[rows(i), :] = dpre
        put(i, dpre_v, dpre_hbm, dpre_sem).start()
        cot_v[rows(i), :] = total + mm_nt(dpre, pin_v[0:L, :])
        put(i, cot_v, egrad_hbm, egrad_sem).start()
        return carry

    lax.fori_loop(0, CHUNKS, backward, 0)
    nout_copy.wait()
    npart_copy.wait()
    gnode_copy.wait()
    for i in range(CHUNKS):
        put(i, enew_v, eout_hbm, eout_sem).wait()
        put(i, hid_v, hid_hbm, hid_sem).wait()
        put(i, draw_v, draw_hbm, draw_sem).wait()
        put(i, dpre_v, dpre_hbm, dpre_sem).wait()
        put(i, cot_v, egrad_hbm, egrad_sem).wait()


def run_rows(n_dom, *operands):
    hbm = pl.BlockSpec(memory_space=pl.ANY)
    vmem = pl.BlockSpec(memory_space=pltpu.VMEM)
    smem = pl.BlockSpec(memory_space=pltpu.SMEM)
    shape = jax.ShapeDtypeStruct
    dma = pltpu.SemaphoreType.DMA
    return pl.pallas_call(
        functools.partial(rows_kernel, n_dom),
        out_shape=[
            shape((N, L), BF),
            shape((E, L), BF),
            shape((E, L), F32),
            shape((E, L), BF),
            shape((E, L), BF),
            shape((E, L), BF),
            shape((16, 96, L), BF),
            shape((N, L), F32),
        ],
        in_specs=[vmem, vmem, smem, hbm, hbm, hbm, hbm, vmem, hbm, vmem, vmem]
        + [hbm, vmem, hbm, vmem, vmem, hbm, hbm],
        out_specs=[hbm] * 8,
        scratch_shapes=[
            pltpu.VMEM((16, 128), I32),
            pltpu.VMEM((E, XW), BF),
            pltpu.VMEM((N, E), BF),
            pltpu.VMEM((XW, L), BF),
            pltpu.VMEM((TAB, L), BF),
            pltpu.VMEM((3 * L, L), BF),
            pltpu.VMEM((L, L), BF),
            pltpu.VMEM((2 * L, L), BF),
            pltpu.VMEM((L, L), BF),
            pltpu.VMEM((N, L), F32),
            pltpu.VMEM((E, L), F32),
            pltpu.VMEM((E, L), F32),
            pltpu.VMEM((E, L), BF),
            pltpu.VMEM((E, L), F32),
            pltpu.VMEM((E, 1), F32),
            pltpu.VMEM((E, L), BF),
            pltpu.VMEM((E, L), BF),
            pltpu.VMEM((E, L), BF),
            pltpu.VMEM((N, 2 * L), BF),
            pltpu.VMEM((N, L), BF),
            pltpu.VMEM((N, L), BF),
            pltpu.VMEM((N, L), F32),
            pltpu.VMEM((16, 96, L), BF),
            dma((7,)),
            dma((CHUNKS,)),
            dma((CHUNKS,)),
            dma((CHUNKS,)),
            dma((CHUNKS,)),
            dma((CHUNKS,)),
            dma((CHUNKS,)),
            dma((CHUNKS,)),
            dma((3,)),
        ],
        compiler_params=pltpu.CompilerParams(vmem_limit_bytes=VMEM_LIMIT),
        name="rows",
    )(*operands)


WIDE = L // 2
LANES = 128


class Wave:
    def __init__(self, coords, refs):
        self.coords = coords
        (self.own, self.from_core, self.a1, self.b1, self.sa, self.sb, self.a2, self.b2) = refs[:8]
        self.send, self.recv = refs[8:]
        self.copies = []

    def start(self, src, dst, k, device):
        copy = pltpu.make_async_remote_copy(
            src_ref=src,
            dst_ref=dst,
            send_sem=self.send.at[k],
            recv_sem=self.recv.at[k],
            device_id=(device,),
            device_id_type=MESH,
        )
        copy.start()
        self.copies.append(copy)

    def to_core(self, src):
        z, x, y, c = self.coords
        self.start(src, self.from_core, 0, device_at(z, x, y, 1 - c))

    def first(self):
        z, x, y, c = self.coords
        self.copies[0].wait_recv()
        own, got = self.own, self.from_core
        for zz in range(4):
            own[zz] = (own[zz].astype(F32) + got[zz].astype(F32)).astype(BF)
        for o in range(1, 4):
            zp, xp = lax.rem(z + 4 - o, 4), lax.rem(x + 4 - o, 4)
            self.start(own.at[zp, :, :, pl.ds(0, LANES)], self.a1.at[o - 1], o, device_at(zp, x, y, c))
            self.start(own.at[:, xp, :, pl.ds(LANES, LANES)], self.b1.at[o - 1], 3 + o, device_at(z, xp, y, c))

    def second(self):
        z, x, y, c = self.coords
        for copy in self.copies[1:7]:
            copy.wait_recv()
        a = self.own[z, :, :, 0:LANES].astype(F32)
        b = self.own[:, x, :, LANES:WIDE].astype(F32)
        for o in range(3):
            a = a + self.a1[o].astype(F32)
            b = b + self.b1[o].astype(F32)
        self.sa[...] = a.astype(BF)
        self.sb[...] = b.astype(BF)
        for o in range(1, 4):
            zp, xp = lax.rem(z + 4 - o, 4), lax.rem(x + 4 - o, 4)
            self.start(self.sa.at[xp], self.a2.at[o - 1], 6 + o, device_at(z, xp, y, c))
            self.start(self.sb.at[zp], self.b2.at[o - 1], 9 + o, device_at(zp, x, y, c))

    def third(self, block, at):
        z, x, y, c = self.coords
        for copy in self.copies[7:13]:
            copy.wait_recv()
        a, b = self.sa[x].astype(F32), self.sb[z].astype(F32)
        for o in range(3):
            a = a + self.a2[o].astype(F32)
            b = b + self.b2[o].astype(F32)
        block[at, 0:LANES] = a.astype(BF)
        block[at, LANES:WIDE] = b.astype(BF)

    def finish(self):
        for copy in self.copies:
            copy.wait_send()


def device_at(z, x, y, c):
    return ((z * 4 + x) * 4 + y) * 2 + c


def wave_scratch(depth):
    dma = pltpu.SemaphoreType.DMA
    return [
        pltpu.VMEM((4, 4, depth, WIDE), BF),
        pltpu.VMEM((4, 4, depth, WIDE), BF),
        pltpu.VMEM((3, 4, depth, LANES), BF),
        pltpu.VMEM((3, 4, depth, LANES), BF),
        pltpu.VMEM((4, depth, LANES), BF),
        pltpu.VMEM((4, depth, LANES), BF),
        pltpu.VMEM((3, depth, LANES), BF),
        pltpu.VMEM((3, depth, LANES), BF),
        dma((13,)),
        dma((13,)),
    ]


def sums_kernel(
    n_dom,
    snd_ref, rcv_ref, gnode_hbm, h_hbm, halo_hbm, e_hbm, pin_hbm, hid_hbm, draw_hbm, dpre_hbm,
    out_ref, part_ref, ret_ref,
    tab_v, e_v, hid_v, draw_v, dpre_v, ps_v, pr_v, st_v, rt_v, as_v, ar_v, there_in, there_out, y_v,
    block, sorted_v, got, in_sem, y_send, y_recv, last_send, last_recv,
    *wave_refs,
):
    me = lax.axis_index("dom")
    c = lax.rem(me, 2)
    y = lax.rem(me // 2, 4)
    x = lax.rem(me // 8, 4)
    z = me // 32
    m = lax.rem(me, 8)
    coords = (z, x, y, c)
    node_wave = Wave(coords, wave_refs[0:10])
    in_wave = Wave(coords, wave_refs[10:20])
    out_wave = Wave(coords, wave_refs[20:30])

    mine = pl.ds(pl.multiple_of(c * WIDE, WIDE), WIDE)
    theirs = pl.ds(pl.multiple_of((1 - c) * WIDE, WIDE), WIDE)
    halves = (theirs, mine)

    loads = []

    def load(src, dst):
        copy = pltpu.make_async_copy(src, dst, in_sem.at[len(loads)])
        copy.start()
        loads.append(copy)

    load(dpre_hbm.at[:, theirs], dpre_v.at[0])
    load(h_hbm, tab_v.at[pl.ds(0, N)])
    load(halo_hbm, tab_v.at[pl.ds(N, HPAD)])
    load(e_hbm, e_v)
    load(dpre_hbm.at[:, mine], dpre_v.at[1])
    for k in range(4):
        load(gnode_hbm.at[pl.ds(4 * k, 4), :, mine], node_wave.own.at[k])
    load(hid_hbm, hid_v)
    load(draw_hbm.at[:, theirs], draw_v.at[0])
    load(draw_hbm.at[:, mine], draw_v.at[1])
    for half in range(2):
        load(pin_hbm.at[pl.ds(L, L), halves[half]], ps_v.at[half])
        load(pin_hbm.at[pl.ds(2 * L, L), halves[half]], pr_v.at[half])

    owners = [lax.rem(me + slot_shift(s) + n_dom, n_dom) for s in range(SLOTS)]
    others = [device_at(z, x, 0, 0) + lax.rem(m + 8 - o, 8) for o in range(1, 8)]
    along = [device_at(lax.rem(z + o, 4), x, y, c) for o in range(1, 4)]
    along += [device_at(z, lax.rem(x + o, 4), y, c) for o in range(1, 4)]
    greet(owners + others + along)

    node_wave.start(
        gnode_hbm.at[:, :, theirs],
        node_wave.from_core.reshape(16, 96, WIDE),
        0,
        device_at(z, x, y, 1 - c),
    )

    index = table_index(snd_ref[...], me, n_dom)
    high = lax.broadcasted_iota(I32, (TAB, 128), 0)
    for k in range(E // 128):
        at = pl.ds(k * 128, 128)
        st_v[:, at] = (jnp.broadcast_to(index[k : k + 1, :], (TAB, 128)) == high).astype(F32).astype(BF)
        rt_v[:, at] = (
            (jnp.broadcast_to(rcv_ref[k : k + 1, :], (N, 128)) == high[0:N, :]).astype(F32).astype(BF)
        )

    for k in range(4):
        loads[k].wait()

    def in_products(half, dst):
        dpre = dpre_v[half]
        sent = mm(st_v[...], dpre).astype(BF)
        taken = mm(rt_v[...], dpre).astype(BF)
        as_v[half] = sent
        ar_v[half] = taken
        product = jnp.concatenate(
            [mm_tn(e_v[...], dpre), mm_tn(tab_v[...], sent), mm_tn(tab_v[0:N, :], taken)], axis=0
        )
        dst[...] = product.astype(BF).reshape(4, 4, 96, WIDE)

    def out_products(half, dst):
        dst[...] = mm_tn(hid_v[...], draw_v[half]).astype(BF).reshape(4, 4, 32, WIDE)

    in_products(0, there_in)
    in_wave.to_core(there_in)
    for k in range(5, 9):
        loads[k].wait()
    node_wave.first()
    loads[4].wait()
    in_products(1, in_wave.own)
    in_wave.first()
    node_wave.second()

    for k in range(9, 16):
        loads[k].wait()
    out_products(0, there_out)
    out_wave.to_core(there_out)
    out_products(1, out_wave.own)

    y_v[...] = mm_nt(as_v[0, N : N + HALO, :], ps_v[0]) + mm_nt(as_v[1, N : N + HALO, :], ps_v[1])
    returns = []
    for s in range(SLOTS):
        copy = pltpu.make_async_remote_copy(
            src_ref=y_v.at[pl.ds(s * HB, HB)],
            dst_ref=ret_ref.at[pl.ds(s * HB, HB)],
            send_sem=y_send.at[s],
            recv_sem=y_recv.at[s],
            device_id=(owners[s],),
            device_id_type=MESH,
        )
        copy.start()
        returns.append(copy)
    out_wave.first()
    part_ref[...] = (
        mm_nt(as_v[0, 0:N, :], ps_v[0])
        + mm_nt(as_v[1, 0:N, :], ps_v[1])
        + mm_nt(ar_v[0], pr_v[0])
        + mm_nt(ar_v[1], pr_v[1])
    ).astype(BF)
    node_wave.third(block, pl.ds(0, 96))
    in_wave.second()
    out_wave.second()
    in_wave.third(block, pl.ds(96, 96))
    out_wave.third(block, pl.ds(192, 32))

    row = lax.broadcasted_iota(I32, (256, 224), 0)
    col = lax.broadcasted_iota(I32, (256, 224), 1)
    j = row // 32
    r = row - j * 32
    source = jnp.where(
        r < 8,
        8 * j + r,
        jnp.where(
            r < 12,
            64 + 4 * j + (r - 8),
            jnp.where(r < 24, 96 + 12 * j + (r - 12), jnp.where(r < 28, 192 + 4 * j + (r - 24), -1)),
        ),
    )
    order = (source == col).astype(F32).astype(BF)
    sorted_v[...] = mm(order, block[...]).astype(BF).reshape(8, 32, WIDE)
    lasts = []
    for o in range(1, 8):
        target = lax.rem(m + 8 - o, 8)
        copy = pltpu.make_async_remote_copy(
            src_ref=sorted_v.at[target],
            dst_ref=got.at[o - 1],
            send_sem=last_send.at[o - 1],
            recv_sem=last_recv.at[o - 1],
            device_id=(others[o - 1],),
            device_id_type=MESH,
        )
        copy.start()
        lasts.append(copy)
    for copy in lasts:
        copy.wait_recv()
    same = sorted_v[m].astype(F32)
    for o in (2, 4, 6):
        same = same + got[o - 1].astype(F32)
    cross = got[0].astype(F32)
    for o in (3, 5, 7):
        cross = cross + got[o - 1].astype(F32)
    even = c == 0
    out_ref[:, 0:WIDE] = jnp.where(even, same, cross)
    out_ref[:, WIDE:] = jnp.where(even, cross, same)
    for copy in returns:
        copy.wait()
    for copy in lasts:
        copy.wait_send()
    for wave in (node_wave, in_wave, out_wave):
        wave.finish()


def run_sums(n_dom, *operands):
    hbm = pl.BlockSpec(memory_space=pl.ANY)
    vmem = pl.BlockSpec(memory_space=pltpu.VMEM)
    shape = jax.ShapeDtypeStruct
    dma = pltpu.SemaphoreType.DMA
    return pl.pallas_call(
        functools.partial(sums_kernel, n_dom),
        out_shape=[shape((32, L), F32), shape((N, L), BF), shape((HALO, L), F32)],
        in_specs=[vmem, vmem] + [hbm] * 8,
        out_specs=[vmem, vmem, vmem],
        scratch_shapes=[
            pltpu.VMEM((TAB, L), BF),
            pltpu.VMEM((E, L), BF),
            pltpu.VMEM((E, L), BF),
            pltpu.VMEM((2, E, WIDE), BF),
            pltpu.VMEM((2, E, WIDE), BF),
            pltpu.VMEM((2, L, WIDE), BF),
            pltpu.VMEM((2, L, WIDE), BF),
            pltpu.VMEM((TAB, E), BF),
            pltpu.VMEM((N, E), BF),
            pltpu.VMEM((2, TAB, WIDE), BF),
            pltpu.VMEM((2, N, WIDE), BF),
            pltpu.VMEM((4, 4, 96, WIDE), BF),
            pltpu.VMEM((4, 4, 32, WIDE), BF),
            pltpu.VMEM((HALO, L), F32),
            pltpu.VMEM((224, WIDE), BF),
            pltpu.VMEM((8, 32, WIDE), BF),
            pltpu.VMEM((7, 32, WIDE), BF),
            dma((16,)),
            dma((SLOTS,)),
            dma((SLOTS,)),
            dma((7,)),
            dma((7,)),
        ]
        + wave_scratch(96)
        + wave_scratch(96)
        + wave_scratch(32),
        compiler_params=pltpu.CompilerParams(
            collective_id=1, has_side_effects=True, vmem_limit_bytes=VMEM_LIMIT
        ),
        name="sums",
    )(*operands)


def last_kernel(
    n_dom, edge_factor, node_factor,
    rows_ref, sums_ref, part_ref, ret_ref, npart_ref,
    grad_ref, ein_ref, eout_ref, nin_ref, nout_ref,
):
    me = lax.axis_index("dom")
    grad_ref[...] = npart_ref[...] + part_ref[...].astype(F32)
    for s in range(SLOTS):
        reader = lax.rem(me - slot_shift(s) + n_dom, n_dom)
        for k in range(HB):
            at = pl.ds(rows_ref[reader * HB + k], 1)
            grad_ref[at, :] = grad_ref[at, :] + ret_ref[s * HB + k : s * HB + k + 1, :]
    nin_ref[0] = sums_ref[0:8, :] * node_factor
    nout_ref[0] = sums_ref[8:12, :] * node_factor
    ein_ref[0] = sums_ref[12:24, :] * edge_factor
    eout_ref[0] = sums_ref[24:28, :] * edge_factor


def run_last(n_dom, edge_factor, node_factor, *operands):
    vmem = pl.BlockSpec(memory_space=pltpu.VMEM)
    smem = pl.BlockSpec(memory_space=pltpu.SMEM)
    shape = jax.ShapeDtypeStruct
    return pl.pallas_call(
        functools.partial(last_kernel, n_dom, edge_factor, node_factor),
        out_shape=[
            shape((N, L), F32),
            shape((1, 12, L), F32),
            shape((1, 4, L), F32),
            shape((1, 8, L), F32),
            shape((1, 4, L), F32),
        ],
        in_specs=[smem, vmem, vmem, vmem, vmem],
        out_specs=[vmem] * 5,
        name="last",
    )(*operands)


def per_device(
    node_latent,
    edge_latent,
    sender_index,
    receiver_index,
    send_rows,
    node_count,
    edge_proj_in,
    edge_bias_in,
    edge_proj_out,
    edge_bias_out,
    edge_gain,
    node_proj_in,
    node_bias_in,
    node_proj_out,
    node_bias_out,
    node_gain,
    node_cot,
    edge_cot,
):
    n_dom = lax.axis_size("dom")
    slot_rows = send_rows.reshape(-1)
    snd = sender_index.reshape(E // 128, 128)
    rcv = receiver_index.reshape(E // 128, 128)
    pin, pout = edge_proj_in.reshape(3 * L, L), edge_proj_out.reshape(L, L)
    halo = fetch_halo(node_latent, slot_rows, n_dom)
    node_out, edge_out, edge_grad, dpre, draw, hid, gnode, npart = run_rows(
        n_dom, snd, rcv, node_count, node_latent, halo, edge_latent, pin, edge_bias_in, pout,
        edge_bias_out, edge_gain, node_proj_in.reshape(2 * L, L), node_bias_in,
        node_proj_out.reshape(L, L), node_bias_out, node_gain, node_cot, edge_cot,
    )
    sums, part, returned = run_sums(
        n_dom, snd, rcv, gnode, node_latent, halo, edge_latent, pin, hid, draw, dpre
    )
    edge_factor = float(E * n_dom) ** (-0.5)
    node_factor = float(N * n_dom) ** (-0.5)
    node_grad, edge_in, edge_out_grad, node_in, node_out_grad = run_last(
        n_dom, edge_factor, node_factor, slot_rows, sums, part, returned, npart
    )
    return node_out, edge_out, node_grad, edge_grad, edge_in, edge_out_grad, node_in, node_out_grad


def solution(mesh):
    rows = P("dom", None)
    one = P("dom")
    whole = P()
    in_specs = (rows, rows, one, one, P("dom", None, None), one) + (whole,) * 10 + (rows, rows)
    split = P(None, "dom", None)
    out_specs = (rows,) * 4 + (split,) * 4
    return jax.shard_map(per_device, mesh=mesh, in_specs=in_specs, out_specs=out_specs, check_vma=False)
```

```python
import functools

import jax
import jax.numpy as jnp
from jax import lax
from jax.experimental import pallas as pl
from jax.experimental.pallas import tpu as pltpu
from jax.sharding import PartitionSpec as P

EPS = 1e-05
MESH = pl.DeviceIdType.MESH
BF = jnp.bfloat16
F32 = jnp.float32
I32 = jnp.int32

L = 512
N = 512
E = 2048
HB = 8
SLOTS = 9
HALO = SLOTS * HB
HPAD = 128
TAB = N + HPAD
C = 512
CHUNKS = E // C
XW = L + TAB + N
WIDE = L // 2
LANES = 128
VMEM_LIMIT = 56 * 1024 * 1024

NT = (((1,), (1,)), ((), ()))
TN = (((0,), (0,)), ((), ()))


def slot_shift(slot):
    return 64 if slot == 4 else slot - 4


def mm(a, b):
    return jnp.dot(a, b, preferred_element_type=F32)


def mm_nt(a, b):
    return lax.dot_general(a, b, NT, preferred_element_type=F32)


def mm_tn(a, b):
    return lax.dot_general(a, b, TN, preferred_element_type=F32)


def sigmoid(x):
    return 0.5 * jnp.tanh(0.5 * x) + 0.5


def table_index(sender, me, n_dom):
    far = sender - N
    peer = far // HB
    row = far - peer * HB
    turn = lax.rem(peer - me + (n_dom + 4), n_dom)
    slot = jnp.where(turn == 68, 4, turn)
    return jnp.where(sender < N, sender, N + slot * HB + row)


def greet(devices):
    barrier = pltpu.get_barrier_semaphore()
    for device in devices:
        pl.semaphore_signal(barrier, inc=1, device_id=(device,), device_id_type=MESH)
    pl.semaphore_wait(barrier, len(devices))


def halo_kernel(n_dom, h_ref, rows_ref, out_ref, wide, outgoing, incoming, send_sem, recv_sem):
    me = lax.axis_index("dom")
    targets = [lax.rem(me - slot_shift(s) + n_dom, n_dom) for s in range(SLOTS)]
    wide[...] = h_ref[...].astype(F32)
    barrier = pltpu.get_barrier_semaphore()
    for device in targets:
        pl.semaphore_signal(barrier, inc=1, device_id=(device,), device_id_type=MESH)
    for s in range(SLOTS):
        for k in range(HB):
            row = rows_ref[k, targets[s]]
            outgoing[pl.ds(s * HB + k, 1), :] = wide[pl.ds(row, 1), :]
    pl.semaphore_wait(barrier, SLOTS)
    copies = []
    for s in range(SLOTS):
        copy = pltpu.make_async_remote_copy(
            src_ref=outgoing.at[pl.ds(s * HB, HB)],
            dst_ref=incoming.at[pl.ds(s * HB, HB)],
            send_sem=send_sem.at[s],
            recv_sem=recv_sem.at[s],
            device_id=(targets[s],),
            device_id_type=MESH,
        )
        copy.start()
        copies.append(copy)
    for copy in copies:
        copy.wait()
    out_ref[...] = jnp.concatenate(
        [incoming[...].astype(BF), jnp.zeros((HPAD - HALO, L), BF)], axis=0
    )


def fetch_halo(node_rows, slot_rows, n_dom):
    return pl.pallas_call(
        functools.partial(halo_kernel, n_dom),
        out_shape=jax.ShapeDtypeStruct((HPAD, L), BF),
        in_specs=[
            pl.BlockSpec(memory_space=pltpu.VMEM),
            pl.BlockSpec(memory_space=pltpu.SMEM),
        ],
        out_specs=pl.BlockSpec(memory_space=pltpu.VMEM),
        scratch_shapes=[
            pltpu.VMEM((N, L), F32),
            pltpu.VMEM((HALO, L), F32),
            pltpu.VMEM((HALO, L), F32),
            pltpu.SemaphoreType.DMA((SLOTS,)),
            pltpu.SemaphoreType.DMA((SLOTS,)),
        ],
        compiler_params=pltpu.CompilerParams(collective_id=0, has_side_effects=True),
        name="halo",
    )(node_rows, slot_rows)


def norm_forward(raw):
    centered = raw - jnp.mean(raw, axis=-1, keepdims=True)
    inv = lax.rsqrt(jnp.mean(centered * centered, axis=-1, keepdims=True) + EPS)
    return centered * inv, inv


def norm_backward(q, normed, inv):
    first = jnp.mean(q, axis=-1, keepdims=True)
    second = jnp.mean(q * normed, axis=-1, keepdims=True)
    return inv * (q - first - normed * second)


def act_slope(pre):
    gate = sigmoid(pre)
    return gate * (1.0 + pre * (1.0 - gate))


def rows_kernel(
    n_dom,
    snd_ref, rcv_ref, cnt_ref, h_hbm, halo_hbm, e_hbm, pin_hbm, b_in, pout_hbm, b_out, gain,
    npin_hbm, nb_in, npout_hbm, nb_out, ngain, ncot_hbm, ecot_hbm,
    nout_hbm, eout_hbm, egrad_hbm, dpre_hbm, draw_hbm, hid_hbm, gnode_hbm, npart_hbm,
    idx_v, x_v, rt_v, w_v, tab_v, pin_v, pout_v, npin_v, npout_v, ncot_v, cot_v,
    pre_v, hid_v, n_v, inv_v, enew_v, draw_v, dpre_v, nx_v, dy_v, nout_v, npart_v, gnode_v,
    in_sem, e_sem, cot_sem, eout_sem, hid_sem, draw_sem, dpre_sem, egrad_sem, out_sem,
):
    me = lax.axis_index("dom")

    def load(k, src, dst):
        return pltpu.make_async_copy(src, dst, in_sem.at[k])

    def rows(i):
        return pl.ds(pl.multiple_of(i * C, C), C)

    def e_load(i):
        return pltpu.make_async_copy(e_hbm.at[rows(i)], x_v.at[rows(i), pl.ds(0, L)], e_sem.at[i])

    def cot_load(i):
        return pltpu.make_async_copy(ecot_hbm.at[rows(i)], cot_v.at[rows(i)], cot_sem.at[i])

    def put(i, src, dst, sem):
        return pltpu.make_async_copy(src.at[rows(i)], dst.at[rows(i)], sem.at[i])

    loads = [
        load(0, h_hbm, tab_v.at[pl.ds(0, N)]),
        load(1, halo_hbm, tab_v.at[pl.ds(N, HPAD)]),
        load(2, pin_hbm, pin_v),
        load(3, pout_hbm, pout_v),
        load(4, npin_hbm, npin_v),
        load(5, npout_hbm, npout_v),
        load(6, ncot_hbm, ncot_v),
    ]
    for k in range(3):
        loads[k].start()
    for i in range(CHUNKS):
        e_load(i).start()
    for k in range(3, 7):
        loads[k].start()
    for i in range(CHUNKS):
        cot_load(i).start()

    idx_v[...] = table_index(snd_ref[...], me, n_dom)
    lane = lax.broadcasted_iota(I32, (128, 128), 1)
    high = lax.broadcasted_iota(I32, (N, 128), 0)

    for k in range(3):
        loads[k].wait()
    w_v[0:L, :] = pin_v[0:L, :]
    w_v[L : L + TAB, :] = mm(tab_v[...], pin_v[L : 2 * L, :]).astype(BF)
    w_v[L + TAB :, :] = (mm(tab_v[0:N, :], pin_v[2 * L :, :]) + b_in[...]).astype(BF)
    loads[3].wait()

    def forward(i, carry):
        e_load(i).wait()
        for b in range(C // 128):
            block = i * (C // 128) + b
            at = pl.ds(pl.multiple_of(block * 128, 128), 128)
            s_col = jnp.broadcast_to(idx_v[pl.ds(block, 1), :], (128, 128)).T
            r_row = rcv_ref[pl.ds(block, 1), :]
            r_col = jnp.broadcast_to(r_row, (128, 128)).T
            for m in range(TAB // 128):
                x_v[at, L + 128 * m : L + 128 * (m + 1)] = (s_col == lane + 128 * m).astype(F32).astype(BF)
            for m in range(N // 128):
                x_v[at, L + TAB + 128 * m : L + TAB + 128 * (m + 1)] = (
                    (r_col == lane + 128 * m).astype(F32).astype(BF)
                )
            rt_v[:, at] = (jnp.broadcast_to(r_row, (N, 128)) == high).astype(F32).astype(BF)
        pre = mm(x_v[rows(i), :], w_v[...])
        pre_v[rows(i), :] = pre
        hid = (pre * sigmoid(pre)).astype(BF)
        hid_v[rows(i), :] = hid
        raw = mm(hid, pout_v[...]) + b_out[...]
        normed, inv = norm_forward(raw)
        n_v[rows(i), :] = normed
        inv_v[rows(i), :] = inv
        enew_v[rows(i), :] = (x_v[rows(i), 0:L].astype(F32) + normed * gain[...]).astype(BF)
        put(i, enew_v, eout_hbm, eout_sem).start()
        put(i, hid_v, hid_hbm, hid_sem).start()
        return carry

    lax.fori_loop(0, CHUNKS, forward, 0)

    valid = (lax.broadcasted_iota(I32, (N, 1), 0) < cnt_ref[0]).astype(F32)
    nx_v[:, 0:L] = tab_v[0:N, :]
    nx_v[:, L:] = (mm(rt_v[...], enew_v[...]) * valid).astype(BF)
    for k in range(4, 7):
        loads[k].wait()
    pre = mm(nx_v[...], npin_v[...]) + nb_in[...]
    hid = (pre * sigmoid(pre)).astype(BF)
    normed, inv = norm_forward(mm(hid, npout_v[...]) + nb_out[...])
    nout_v[...] = (tab_v[0:N, :].astype(F32) + valid * (normed * ngain[...])).astype(BF)
    nout_copy = pltpu.make_async_copy(nout_v, nout_hbm, out_sem.at[0])
    nout_copy.start()
    draw = norm_backward(valid * ncot_v[...] * ngain[...], normed, inv).astype(BF)
    dpre = (mm_nt(draw, npout_v[...]) * act_slope(pre)).astype(BF)
    npart_v[...] = ncot_v[...] + mm_nt(dpre, npin_v[0:L, :])
    npart_copy = pltpu.make_async_copy(npart_v, npart_hbm, out_sem.at[1])
    npart_copy.start()
    dy_v[...] = mm_nt(dpre, npin_v[L:, :]).astype(BF)
    grad_in = mm_tn(nx_v[...], dpre).astype(BF)
    grad_out = mm_tn(hid, draw).astype(BF)
    for k in range(4):
        columns = slice(LANES * k, LANES * (k + 1))
        gnode_v[k, :, 0:64, :] = grad_in[:, columns].reshape(16, 64, LANES)
        gnode_v[k, :, 64:96, :] = grad_out[:, columns].reshape(16, 32, LANES)
    gnode_copy = pltpu.make_async_copy(gnode_v, gnode_hbm, out_sem.at[2])
    gnode_copy.start()

    def backward(i, carry):
        cot_load(i).wait()
        total = cot_v[rows(i), :] + mm(x_v[rows(i), L + TAB :], dy_v[...])
        draw = norm_backward(total * gain[...], n_v[rows(i), :], inv_v[rows(i), :]).astype(BF)
        draw_v[rows(i), :] = draw
        put(i, draw_v, draw_hbm, draw_sem).start()
        dpre = (mm_nt(draw, pout_v[...]) * act_slope(pre_v[rows(i), :])).astype(BF)
        dpre_v[rows(i), :] = dpre
        put(i, dpre_v, dpre_hbm, dpre_sem).start()
        cot_v[rows(i), :] = total + mm_nt(dpre, pin_v[0:L, :])
        put(i, cot_v, egrad_hbm, egrad_sem).start()
        return carry

    lax.fori_loop(0, CHUNKS, backward, 0)
    nout_copy.wait()
    npart_copy.wait()
    gnode_copy.wait()
    for i in range(CHUNKS):
        put(i, enew_v, eout_hbm, eout_sem).wait()
        put(i, hid_v, hid_hbm, hid_sem).wait()
        put(i, draw_v, draw_hbm, draw_sem).wait()
        put(i, dpre_v, dpre_hbm, dpre_sem).wait()
        put(i, cot_v, egrad_hbm, egrad_sem).wait()


def run_rows(n_dom, *operands):
    hbm = pl.BlockSpec(memory_space=pl.ANY)
    vmem = pl.BlockSpec(memory_space=pltpu.VMEM)
    smem = pl.BlockSpec(memory_space=pltpu.SMEM)
    shape = jax.ShapeDtypeStruct
    dma = pltpu.SemaphoreType.DMA
    return pl.pallas_call(
        functools.partial(rows_kernel, n_dom),
        out_shape=[
            shape((N, L), BF),
            shape((E, L), BF),
            shape((E, L), F32),
            shape((E, L), BF),
            shape((E, L), BF),
            shape((E, L), BF),
            shape((4, 16, 96, LANES), BF),
            shape((N, L), F32),
        ],
        in_specs=[vmem, vmem, smem, hbm, hbm, hbm, hbm, vmem, hbm, vmem, vmem]
        + [hbm, vmem, hbm, vmem, vmem, hbm, hbm],
        out_specs=[hbm] * 8,
        scratch_shapes=[
            pltpu.VMEM((16, 128), I32),
            pltpu.VMEM((E, XW), BF),
            pltpu.VMEM((N, E), BF),
            pltpu.VMEM((XW, L), BF),
            pltpu.VMEM((TAB, L), BF),
            pltpu.VMEM((3 * L, L), BF),
            pltpu.VMEM((L, L), BF),
            pltpu.VMEM((2 * L, L), BF),
            pltpu.VMEM((L, L), BF),
            pltpu.VMEM((N, L), F32),
            pltpu.VMEM((E, L), F32),
            pltpu.VMEM((E, L), F32),
            pltpu.VMEM((E, L), BF),
            pltpu.VMEM((E, L), F32),
            pltpu.VMEM((E, 1), F32),
            pltpu.VMEM((E, L), BF),
            pltpu.VMEM((E, L), BF),
            pltpu.VMEM((E, L), BF),
            pltpu.VMEM((N, 2 * L), BF),
            pltpu.VMEM((N, L), BF),
            pltpu.VMEM((N, L), BF),
            pltpu.VMEM((N, L), F32),
            pltpu.VMEM((4, 16, 96, LANES), BF),
            dma((7,)),
            dma((CHUNKS,)),
            dma((CHUNKS,)),
            dma((CHUNKS,)),
            dma((CHUNKS,)),
            dma((CHUNKS,)),
            dma((CHUNKS,)),
            dma((CHUNKS,)),
            dma((3,)),
        ],
        compiler_params=pltpu.CompilerParams(vmem_limit_bytes=VMEM_LIMIT),
        name="rows",
    )(*operands)


class Wave:
    def __init__(self, coords, refs):
        self.coords = coords
        (self.own, self.from_core, self.near, self.next, self.sa, self.sb, self.a2, self.b2) = refs[:8]
        self.send, self.recv = refs[8:]
        self.copies = []

    def start(self, src, dst, device):
        k = len(self.copies)
        copy = pltpu.make_async_remote_copy(
            src_ref=src,
            dst_ref=dst,
            send_sem=self.send.at[k],
            recv_sem=self.recv.at[k],
            device_id=(device,),
            device_id_type=MESH,
        )
        copy.start()
        self.copies.append(copy)

    def pieces(self, k):
        z, x, y, c = self.coords
        half = pl.ds(2 * (k % 2), 2)
        if k // 2 == 0:
            place, view = z, lambda p: (0, p, half)
            device = lambda p: device_at(p, x, y, c)
        else:
            place, view = x, lambda p: (1, half, p)
            device = lambda p: device_at(z, p, y, c)
        low = lax.rem(place, 2)
        pair = place + 1 - 2 * low
        cross = lax.rem(place + 3 + 2 * low, 4)
        near, far = (pair, cross) if k % 2 == 0 else (cross, pair)
        return view, device, place, near, far

    def to_core(self, src, into=None):
        z, x, y, c = self.coords
        self.start(src, self.from_core if into is None else into, device_at(z, x, y, 1 - c))

    def first(self):
        self.copies[0].wait_recv()
        own, got = self.own, self.from_core
        for lanes in range(2):
            for zz in range(4):
                own[lanes, zz] = (own[lanes, zz].astype(F32) + got[lanes, zz].astype(F32)).astype(BF)
        for k in range(4):
            view, device, place, near, far = self.pieces(k)
            self.start(own.at[view(near)], self.near.at[k, 0], device(near))
            self.start(own.at[view(lax.rem(place + 2, 4))], self.near.at[k, 1], device(near))

    def second(self):
        own = self.own
        for k in range(4):
            view, device, place, near, far = self.pieces(k)
            self.copies[2 + 2 * k].wait_recv()
            own[view(far)] = (own[view(far)].astype(F32) + self.near[k, 1].astype(F32)).astype(BF)
            self.start(own.at[view(far)], self.next.at[k], device(far))

    def third(self):
        z, x, y, c = self.coords
        for k in range(4):
            view, device, place, near, far = self.pieces(k)
            self.copies[1 + 2 * k].wait_recv()
            self.copies[9 + k].wait_recv()
            total = self.own[view(place)].astype(F32) + self.near[k, 0].astype(F32) + self.next[k].astype(F32)
            into = self.sa if k // 2 == 0 else self.sb
            into[2 * (k % 2) : 2 * (k % 2) + 2] = total.astype(BF)
        for o in range(1, 4):
            zp, xp = lax.rem(z + 4 - o, 4), lax.rem(x + 4 - o, 4)
            self.start(self.sa.at[xp], self.a2.at[o - 1], device_at(z, xp, y, c))
            self.start(self.sb.at[zp], self.b2.at[o - 1], device_at(zp, x, y, c))

    def fourth(self, block, at):
        z, x, y, c = self.coords
        for copy in self.copies[13:19]:
            copy.wait_recv()
        a, b = self.sa[x].astype(F32), self.sb[z].astype(F32)
        for o in range(3):
            a = a + self.a2[o].astype(F32)
            b = b + self.b2[o].astype(F32)
        block[at, 0:LANES] = a.astype(BF)
        block[at, LANES:WIDE] = b.astype(BF)

    def finish(self):
        for copy in self.copies:
            copy.wait_send()


def device_at(z, x, y, c):
    return ((z * 4 + x) * 4 + y) * 2 + c


def wave_scratch(depth):
    dma = pltpu.SemaphoreType.DMA
    return [
        pltpu.VMEM((2, 4, 4, depth, LANES), BF),
        pltpu.VMEM((2, 4, 4, depth, LANES), BF),
        pltpu.VMEM((4, 2, 2, depth, LANES), BF),
        pltpu.VMEM((4, 2, depth, LANES), BF),
        pltpu.VMEM((4, depth, LANES), BF),
        pltpu.VMEM((4, depth, LANES), BF),
        pltpu.VMEM((3, depth, LANES), BF),
        pltpu.VMEM((3, depth, LANES), BF),
        dma((19,)),
        dma((19,)),
    ]


def sums_kernel(
    n_dom,
    snd_ref, rcv_ref, gnode_hbm, h_hbm, halo_hbm, e_hbm, pin_hbm, hid_hbm, draw_hbm, dpre_hbm,
    out_ref, part_ref, ret_ref,
    tab_v, e_v, hid_v, draw_v, dpre_v, ps_v, pr_v, st_v, rt_v, as_v, ar_v, there_in, there_out, y_v,
    block, sorted_v, got, in_sem, y_send, y_recv, last_send, last_recv,
    *wave_refs,
):
    me = lax.axis_index("dom")
    c = lax.rem(me, 2)
    y = lax.rem(me // 2, 4)
    x = lax.rem(me // 8, 4)
    z = me // 32
    m = lax.rem(me, 8)
    coords = (z, x, y, c)
    node_wave = Wave(coords, wave_refs[0:10])
    in_wave = Wave(coords, wave_refs[10:20])
    out_wave = Wave(coords, wave_refs[20:30])

    mine = pl.ds(pl.multiple_of(c * WIDE, WIDE), WIDE)
    theirs = pl.ds(pl.multiple_of((1 - c) * WIDE, WIDE), WIDE)
    halves = (theirs, mine)

    loads = []

    def load(src, dst):
        copy = pltpu.make_async_copy(src, dst, in_sem.at[len(loads)])
        copy.start()
        loads.append(copy)

    load(dpre_hbm.at[:, theirs], dpre_v.at[0])
    load(h_hbm, tab_v.at[pl.ds(0, N)])
    load(halo_hbm, tab_v.at[pl.ds(N, HPAD)])
    load(e_hbm, e_v)
    load(dpre_hbm.at[:, mine], dpre_v.at[1])
    for lanes in range(2):
        for k in range(4):
            load(gnode_hbm.at[2 * c + lanes, pl.ds(4 * k, 4)], node_wave.own.at[lanes, k])
    load(hid_hbm, hid_v)
    load(draw_hbm.at[:, theirs], draw_v.at[0])
    load(draw_hbm.at[:, mine], draw_v.at[1])
    for half in range(2):
        load(pin_hbm.at[pl.ds(L, L), halves[half]], ps_v.at[half])
        load(pin_hbm.at[pl.ds(2 * L, L), halves[half]], pr_v.at[half])

    owners = [lax.rem(me + slot_shift(s) + n_dom, n_dom) for s in range(SLOTS)]
    others = [device_at(z, x, 0, 0) + lax.rem(m + 8 - o, 8) for o in range(1, 8)]
    along = [device_at(lax.rem(z + o, 4), x, y, c) for o in range(1, 4)]
    along += [device_at(z, lax.rem(x + o, 4), y, c) for o in range(1, 4)]
    greet(owners + others + along)

    node_wave.to_core(gnode_hbm.at[pl.ds(2 * (1 - c), 2)], node_wave.from_core.reshape(2, 16, 96, LANES))

    index = table_index(snd_ref[...], me, n_dom)
    high = lax.broadcasted_iota(I32, (TAB, 128), 0)
    for k in range(E // 128):
        at = pl.ds(k * 128, 128)
        st_v[:, at] = (jnp.broadcast_to(index[k : k + 1, :], (TAB, 128)) == high).astype(F32).astype(BF)
        rt_v[:, at] = (
            (jnp.broadcast_to(rcv_ref[k : k + 1, :], (N, 128)) == high[0:N, :]).astype(F32).astype(BF)
        )

    for k in range(4):
        loads[k].wait()

    def put_lanes(product, dst, depth):
        for lanes in range(2):
            part = product[:, LANES * lanes : LANES * (lanes + 1)]
            dst[lanes] = part.astype(BF).reshape(4, 4, depth, LANES)

    def in_products(half, dst):
        dpre = dpre_v[half]
        sent = mm(st_v[...], dpre).astype(BF)
        taken = mm(rt_v[...], dpre).astype(BF)
        as_v[half] = sent
        ar_v[half] = taken
        product = jnp.concatenate(
            [mm_tn(e_v[...], dpre), mm_tn(tab_v[...], sent), mm_tn(tab_v[0:N, :], taken)], axis=0
        )
        put_lanes(product, dst, 96)

    def out_products(half, dst):
        put_lanes(mm_tn(hid_v[...], draw_v[half]), dst, 32)

    in_products(0, there_in)
    in_wave.to_core(there_in)
    for k in range(5, 13):
        loads[k].wait()
    node_wave.first()
    loads[4].wait()
    in_products(1, in_wave.own)
    in_wave.first()
    node_wave.second()

    for k in range(13, 20):
        loads[k].wait()
    out_products(0, there_out)
    out_wave.to_core(there_out)
    node_wave.third()
    in_wave.second()
    out_products(1, out_wave.own)
    out_wave.first()

    y_v[...] = mm_nt(as_v[0, N : N + HALO, :], ps_v[0]) + mm_nt(as_v[1, N : N + HALO, :], ps_v[1])
    returns = []
    for s in range(SLOTS):
        copy = pltpu.make_async_remote_copy(
            src_ref=y_v.at[pl.ds(s * HB, HB)],
            dst_ref=ret_ref.at[pl.ds(s * HB, HB)],
            send_sem=y_send.at[s],
            recv_sem=y_recv.at[s],
            device_id=(owners[s],),
            device_id_type=MESH,
        )
        copy.start()
        returns.append(copy)
    in_wave.third()
    out_wave.second()
    part_ref[...] = (
        mm_nt(as_v[0, 0:N, :], ps_v[0])
        + mm_nt(as_v[1, 0:N, :], ps_v[1])
        + mm_nt(ar_v[0], pr_v[0])
        + mm_nt(ar_v[1], pr_v[1])
    ).astype(BF)
    out_wave.third()
    node_wave.fourth(block, pl.ds(0, 96))
    in_wave.fourth(block, pl.ds(96, 96))
    out_wave.fourth(block, pl.ds(192, 32))

    row = lax.broadcasted_iota(I32, (256, 224), 0)
    col = lax.broadcasted_iota(I32, (256, 224), 1)
    j = row // 32
    r = row - j * 32
    source = jnp.where(
        r < 8,
        8 * j + r,
        jnp.where(
            r < 12,
            64 + 4 * j + (r - 8),
            jnp.where(r < 24, 96 + 12 * j + (r - 12), jnp.where(r < 28, 192 + 4 * j + (r - 24), -1)),
        ),
    )
    order = (source == col).astype(F32).astype(BF)
    sorted_v[...] = mm(order, block[...]).astype(BF).reshape(8, 32, WIDE)
    lasts = []
    for o in range(1, 8):
        target = lax.rem(m + 8 - o, 8)
        copy = pltpu.make_async_remote_copy(
            src_ref=sorted_v.at[target],
            dst_ref=got.at[o - 1],
            send_sem=last_send.at[o - 1],
            recv_sem=last_recv.at[o - 1],
            device_id=(others[o - 1],),
            device_id_type=MESH,
        )
        copy.start()
        lasts.append(copy)
    for copy in lasts:
        copy.wait_recv()
    same = sorted_v[m].astype(F32)
    for o in (2, 4, 6):
        same = same + got[o - 1].astype(F32)
    cross = got[0].astype(F32)
    for o in (3, 5, 7):
        cross = cross + got[o - 1].astype(F32)
    even = c == 0
    out_ref[:, 0:WIDE] = jnp.where(even, same, cross)
    out_ref[:, WIDE:] = jnp.where(even, cross, same)
    for copy in returns:
        copy.wait()
    for copy in lasts:
        copy.wait_send()
    for wave in (node_wave, in_wave, out_wave):
        wave.finish()


def run_sums(n_dom, *operands):
    hbm = pl.BlockSpec(memory_space=pl.ANY)
    vmem = pl.BlockSpec(memory_space=pltpu.VMEM)
    shape = jax.ShapeDtypeStruct
    dma = pltpu.SemaphoreType.DMA
    return pl.pallas_call(
        functools.partial(sums_kernel, n_dom),
        out_shape=[shape((32, L), F32), shape((N, L), BF), shape((HALO, L), F32)],
        in_specs=[vmem, vmem] + [hbm] * 8,
        out_specs=[vmem, vmem, vmem],
        scratch_shapes=[
            pltpu.VMEM((TAB, L), BF),
            pltpu.VMEM((E, L), BF),
            pltpu.VMEM((E, L), BF),
            pltpu.VMEM((2, E, WIDE), BF),
            pltpu.VMEM((2, E, WIDE), BF),
            pltpu.VMEM((2, L, WIDE), BF),
            pltpu.VMEM((2, L, WIDE), BF),
            pltpu.VMEM((TAB, E), BF),
            pltpu.VMEM((N, E), BF),
            pltpu.VMEM((2, TAB, WIDE), BF),
            pltpu.VMEM((2, N, WIDE), BF),
            pltpu.VMEM((2, 4, 4, 96, LANES), BF),
            pltpu.VMEM((2, 4, 4, 32, LANES), BF),
            pltpu.VMEM((HALO, L), F32),
            pltpu.VMEM((224, WIDE), BF),
            pltpu.VMEM((8, 32, WIDE), BF),
            pltpu.VMEM((7, 32, WIDE), BF),
            dma((20,)),
            dma((SLOTS,)),
            dma((SLOTS,)),
            dma((7,)),
            dma((7,)),
        ]
        + wave_scratch(96)
        + wave_scratch(96)
        + wave_scratch(32),
        compiler_params=pltpu.CompilerParams(
            collective_id=1, has_side_effects=True, vmem_limit_bytes=VMEM_LIMIT
        ),
        name="sums",
    )(*operands)


def last_kernel(
    n_dom, edge_factor, node_factor,
    rows_ref, sums_ref, part_ref, ret_ref, npart_ref,
    grad_ref, ein_ref, eout_ref, nin_ref, nout_ref,
):
    me = lax.axis_index("dom")
    grad_ref[...] = npart_ref[...] + part_ref[...].astype(F32)
    for s in range(SLOTS):
        reader = lax.rem(me - slot_shift(s) + n_dom, n_dom)
        for k in range(HB):
            at = pl.ds(rows_ref[k, reader], 1)
            grad_ref[at, :] = grad_ref[at, :] + ret_ref[s * HB + k : s * HB + k + 1, :]
    nin_ref[0] = sums_ref[0:8, :] * node_factor
    nout_ref[0] = sums_ref[8:12, :] * node_factor
    ein_ref[...] = (sums_ref[12:24, :] * edge_factor).reshape(12, 1, L)
    eout_ref[0] = sums_ref[24:28, :] * edge_factor


def run_last(n_dom, edge_factor, node_factor, *operands):
    vmem = pl.BlockSpec(memory_space=pltpu.VMEM)
    smem = pl.BlockSpec(memory_space=pltpu.SMEM)
    shape = jax.ShapeDtypeStruct
    return pl.pallas_call(
        functools.partial(last_kernel, n_dom, edge_factor, node_factor),
        out_shape=[
            shape((N, L), F32),
            shape((12, 1, L), F32),
            shape((1, 4, L), F32),
            shape((1, 8, L), F32),
            shape((1, 4, L), F32),
        ],
        in_specs=[smem, vmem, vmem, vmem, vmem],
        out_specs=[vmem] * 5,
        name="last",
    )(*operands)


def per_device(
    node_latent,
    edge_latent,
    sender_index,
    receiver_index,
    send_rows,
    node_count,
    edge_proj_in,
    edge_bias_in,
    edge_proj_out,
    edge_bias_out,
    edge_gain,
    node_proj_in,
    node_bias_in,
    node_proj_out,
    node_bias_out,
    node_gain,
    node_cot,
    edge_cot,
):
    n_dom = lax.axis_size("dom")
    slot_rows = send_rows.transpose(0, 2, 1).reshape(HB, n_dom)
    snd = sender_index.reshape(E // 128, 128)
    rcv = receiver_index.reshape(E // 128, 128)
    pin, pout = edge_proj_in.reshape(3 * L, L), edge_proj_out.reshape(L, L)
    halo = fetch_halo(node_latent, slot_rows, n_dom)
    node_out, edge_out, edge_grad, dpre, draw, hid, gnode, npart = run_rows(
        n_dom, snd, rcv, node_count, node_latent, halo, edge_latent, pin, edge_bias_in, pout,
        edge_bias_out, edge_gain, node_proj_in.reshape(2 * L, L), node_bias_in,
        node_proj_out.reshape(L, L), node_bias_out, node_gain, node_cot, edge_cot,
    )
    sums, part, returned = run_sums(
        n_dom, snd, rcv, gnode, node_latent, halo, edge_latent, pin, hid, draw, dpre
    )
    edge_factor = float(E * n_dom) ** (-0.5)
    node_factor = float(N * n_dom) ** (-0.5)
    node_grad, edge_in, edge_out_grad, node_in, node_out_grad = run_last(
        n_dom, edge_factor, node_factor, slot_rows, sums, part, returned, npart
    )
    edge_in = edge_in.transpose(1, 0, 2)
    return node_out, edge_out, node_grad, edge_grad, edge_in, edge_out_grad, node_in, node_out_grad


def solution(mesh):
    rows = P("dom", None)
    one = P("dom")
    whole = P()
    in_specs = (rows, rows, one, one, P("dom", None, None), one) + (whole,) * 10 + (rows, rows)
    split = P(None, "dom", None)
    out_specs = (rows,) * 4 + (split,) * 4
    return jax.shard_map(per_device, mesh=mesh, in_specs=in_specs, out_specs=out_specs, check_vma=False)
```

```python
import functools

import jax
import jax.numpy as jnp
from jax import lax
from jax.experimental import pallas as pl
from jax.experimental.pallas import tpu as pltpu
from jax.sharding import PartitionSpec as P

EPS = 1e-05
MESH = pl.DeviceIdType.MESH
BF = jnp.bfloat16
F32 = jnp.float32
I32 = jnp.int32

L = 512
N = 512
E = 2048
HB = 8
SLOTS = 9
HALO = SLOTS * HB
HPAD = 128
TAB = N + HPAD
C = 512
CHUNKS = E // C
WIDE = L // 2
LANES = 128
VMEM_LIMIT = 56 * 1024 * 1024

NT = (((1,), (1,)), ((), ()))
TN = (((0,), (0,)), ((), ()))


def slot_shift(slot):
    return 64 if slot == 4 else slot - 4


def mm(a, b):
    return jnp.dot(a, b, preferred_element_type=F32)


def mm_nt(a, b):
    return lax.dot_general(a, b, NT, preferred_element_type=F32)


def mm_tn(a, b):
    return lax.dot_general(a, b, TN, preferred_element_type=F32)


def sigmoid(x):
    return 0.5 * jnp.tanh(0.5 * x) + 0.5


def table_index(sender, me, n_dom):
    far = sender - N
    peer = far // HB
    row = far - peer * HB
    turn = lax.rem(peer - me + (n_dom + 4), n_dom)
    slot = jnp.where(turn == 68, 4, turn)
    return jnp.where(sender < N, sender, N + slot * HB + row)


def greet(devices):
    barrier = pltpu.get_barrier_semaphore()
    for device in devices:
        pl.semaphore_signal(barrier, inc=1, device_id=(device,), device_id_type=MESH)
    pl.semaphore_wait(barrier, len(devices))


def one_hot_columns(index, lane, blocks):
    column = jnp.broadcast_to(index, (128, 128)).T
    return jnp.concatenate(
        [(column == lane + 128 * m).astype(F32).astype(BF) for m in range(blocks)], axis=1
    )


def halo_kernel(
    n_dom,
    snd_ref, rcv_ref, rows_ref, h_hbm, e_hbm, pin_hbm, b_in,
    halo_ref, thalo_ref, pre_hbm,
    h_v, x_v, pin_v, t_v, pre_v, wide, outgoing, incoming,
    in_sem, e_sem, pre_sem, send_sem, recv_sem,
):
    me = lax.axis_index("dom")
    targets = [lax.rem(me - slot_shift(s) + n_dom, n_dom) for s in range(SLOTS)]

    def rows(i):
        return pl.ds(pl.multiple_of(i * C, C), C)

    def e_load(i):
        return pltpu.make_async_copy(e_hbm.at[rows(i)], x_v.at[rows(i), pl.ds(0, L)], e_sem.at[i])

    def pre_put(i):
        return pltpu.make_async_copy(pre_v.at[rows(i)], pre_hbm.at[rows(i)], pre_sem.at[i])

    barrier = pltpu.get_barrier_semaphore()
    for device in targets:
        pl.semaphore_signal(barrier, inc=1, device_id=(device,), device_id_type=MESH)
    h_load = pltpu.make_async_copy(h_hbm, h_v, in_sem.at[0])
    h_load.start()
    pin_load = pltpu.make_async_copy(pin_hbm, pin_v, in_sem.at[1])
    pin_load.start()
    for i in range(CHUNKS):
        e_load(i).start()
    h_load.wait()
    wide[...] = h_v[...].astype(F32)
    for s in range(SLOTS):
        for k in range(HB):
            row = rows_ref[k, targets[s]]
            outgoing[pl.ds(s * HB + k, 1), :] = wide[pl.ds(row, 1), :]
    pl.semaphore_wait(barrier, SLOTS)
    copies = []
    for s in range(SLOTS):
        copy = pltpu.make_async_remote_copy(
            src_ref=outgoing.at[pl.ds(s * HB, HB)],
            dst_ref=incoming.at[pl.ds(s * HB, HB)],
            send_sem=send_sem.at[s],
            recv_sem=recv_sem.at[s],
            device_id=(targets[s],),
            device_id_type=MESH,
        )
        copy.start()
        copies.append(copy)

    pin_load.wait()
    t_v[0:L, :] = pin_v[0:L, :]
    t_v[L : 2 * L, :] = mm(h_v[...], pin_v[L : 2 * L, :]).astype(BF)
    t_v[2 * L :, :] = (mm(h_v[...], pin_v[2 * L :, :]) + b_in[...]).astype(BF)
    lane = lax.broadcasted_iota(I32, (128, 128), 1)

    def local(i, carry):
        for b in range(C // 128):
            block = i * (C // 128) + b
            at = pl.ds(pl.multiple_of(block * 128, 128), 128)
            x_v[at, L : 2 * L] = one_hot_columns(snd_ref[pl.ds(block, 1), :], lane, N // 128)
            x_v[at, 2 * L :] = one_hot_columns(rcv_ref[pl.ds(block, 1), :], lane, N // 128)
        e_load(i).wait()
        pre_v[rows(i), :] = mm(x_v[rows(i), :], t_v[...]).astype(BF)
        pre_put(i).start()
        return carry

    lax.fori_loop(0, CHUNKS, local, 0)
    for copy in copies:
        copy.wait()
    halo = jnp.concatenate([incoming[...].astype(BF), jnp.zeros((HPAD - HALO, L), BF)], axis=0)
    halo_ref[...] = halo
    thalo_ref[...] = mm(halo, pin_v[L : 2 * L, :]).astype(BF)
    for i in range(CHUNKS):
        pre_put(i).wait()


def run_halo(n_dom, *operands):
    hbm = pl.BlockSpec(memory_space=pl.ANY)
    vmem = pl.BlockSpec(memory_space=pltpu.VMEM)
    smem = pl.BlockSpec(memory_space=pltpu.SMEM)
    shape = jax.ShapeDtypeStruct
    dma = pltpu.SemaphoreType.DMA
    return pl.pallas_call(
        functools.partial(halo_kernel, n_dom),
        out_shape=[shape((HPAD, L), BF), shape((HPAD, L), BF), shape((E, L), BF)],
        in_specs=[vmem, vmem, smem, hbm, hbm, hbm, vmem],
        out_specs=[vmem, vmem, hbm],
        scratch_shapes=[
            pltpu.VMEM((N, L), BF),
            pltpu.VMEM((E, 3 * L), BF),
            pltpu.VMEM((3 * L, L), BF),
            pltpu.VMEM((3 * L, L), BF),
            pltpu.VMEM((E, L), BF),
            pltpu.VMEM((N, L), F32),
            pltpu.VMEM((HALO, L), F32),
            pltpu.VMEM((HALO, L), F32),
            dma((2,)),
            dma((CHUNKS,)),
            dma((CHUNKS,)),
            dma((SLOTS,)),
            dma((SLOTS,)),
        ],
        compiler_params=pltpu.CompilerParams(
            collective_id=0, has_side_effects=True, vmem_limit_bytes=VMEM_LIMIT
        ),
        name="halo",
    )(*operands)


def norm_forward(raw):
    centered = raw - jnp.mean(raw, axis=-1, keepdims=True)
    inv = lax.rsqrt(jnp.mean(centered * centered, axis=-1, keepdims=True) + EPS)
    return centered * inv, inv


def norm_backward(q, normed, inv):
    first = jnp.mean(q, axis=-1, keepdims=True)
    second = jnp.mean(q * normed, axis=-1, keepdims=True)
    return inv * (q - first - normed * second)


def act_slope(pre):
    gate = sigmoid(pre)
    return gate * (1.0 + pre * (1.0 - gate))


def rows_kernel(
    n_dom,
    snd_ref, rcv_ref, cnt_ref, thalo_ref, h_hbm, part_hbm, e_hbm, pin_hbm, pout_hbm, b_out, gain,
    npin_hbm, nb_in, npout_hbm, nb_out, ngain, ncot_hbm, ecot_hbm,
    nout_hbm, eout_hbm, egrad_hbm, dpre_hbm, draw_hbm, hid_hbm, gnode_hbm, npart_hbm,
    idx_v, x_v, rt_v, e_v, part_v, h_v, pe_v, pout_v, npin_v, npout_v, ncot_v, cot_v,
    pre_v, hid_v, n_v, inv_v, enew_v, draw_v, dpre_v, nx_v, dy_v, nout_v, npart_v, gnode_v,
    in_sem, e_sem, part_sem, cot_sem, eout_sem, hid_sem, draw_sem, dpre_sem, egrad_sem, out_sem,
):
    me = lax.axis_index("dom")

    def load(k, src, dst):
        return pltpu.make_async_copy(src, dst, in_sem.at[k])

    def rows(i):
        return pl.ds(pl.multiple_of(i * C, C), C)

    def e_load(i):
        return pltpu.make_async_copy(e_hbm.at[rows(i)], e_v.at[rows(i)], e_sem.at[i])

    def part_load(i):
        return pltpu.make_async_copy(part_hbm.at[rows(i)], part_v.at[rows(i)], part_sem.at[i])

    def cot_load(i):
        return pltpu.make_async_copy(ecot_hbm.at[rows(i)], cot_v.at[rows(i)], cot_sem.at[i])

    def put(i, src, dst, sem):
        return pltpu.make_async_copy(src.at[rows(i)], dst.at[rows(i)], sem.at[i])

    loads = [
        load(0, pout_hbm, pout_v),
        load(1, h_hbm, h_v),
        load(2, npin_hbm, npin_v),
        load(3, npout_hbm, npout_v),
        load(4, ncot_hbm, ncot_v),
        load(5, pin_hbm.at[pl.ds(0, L)], pe_v),
    ]
    part_load(0).start()
    loads[0].start()
    for i in range(CHUNKS):
        e_load(i).start()
        if i + 1 < CHUNKS:
            part_load(i + 1).start()
    for k in range(1, 6):
        loads[k].start()
    for i in range(CHUNKS):
        cot_load(i).start()

    idx_v[...] = table_index(snd_ref[...], me, n_dom)
    lane = lax.broadcasted_iota(I32, (128, 128), 1)
    high = lax.broadcasted_iota(I32, (N, 128), 0)
    loads[0].wait()

    def forward(i, carry):
        for b in range(C // 128):
            block = i * (C // 128) + b
            at = pl.ds(pl.multiple_of(block * 128, 128), 128)
            r_row = rcv_ref[pl.ds(block, 1), :]
            x_v[at, 0:HPAD] = one_hot_columns(idx_v[pl.ds(block, 1), :] - N, lane, 1)
            x_v[at, HPAD:] = one_hot_columns(r_row, lane, N // 128)
            rt_v[:, at] = (jnp.broadcast_to(r_row, (N, 128)) == high).astype(F32).astype(BF)
        part_load(i).wait()
        pre = part_v[rows(i), :].astype(F32) + mm(x_v[rows(i), 0:HPAD], thalo_ref[...])
        pre_v[rows(i), :] = pre
        hid = (pre * sigmoid(pre)).astype(BF)
        hid_v[rows(i), :] = hid
        raw = mm(hid, pout_v[...]) + b_out[...]
        normed, inv = norm_forward(raw)
        n_v[rows(i), :] = normed
        inv_v[rows(i), :] = inv
        e_load(i).wait()
        enew_v[rows(i), :] = (e_v[rows(i), :].astype(F32) + normed * gain[...]).astype(BF)
        put(i, enew_v, eout_hbm, eout_sem).start()
        put(i, hid_v, hid_hbm, hid_sem).start()
        return carry

    lax.fori_loop(0, CHUNKS, forward, 0)

    valid = (lax.broadcasted_iota(I32, (N, 1), 0) < cnt_ref[0]).astype(F32)
    nx_v[:, L:] = (mm(rt_v[...], enew_v[...]) * valid).astype(BF)
    for k in range(1, 6):
        loads[k].wait()
    nx_v[:, 0:L] = h_v[...]
    pre = mm(nx_v[...], npin_v[...]) + nb_in[...]
    hid = (pre * sigmoid(pre)).astype(BF)
    normed, inv = norm_forward(mm(hid, npout_v[...]) + nb_out[...])
    nout_v[...] = (h_v[...].astype(F32) + valid * (normed * ngain[...])).astype(BF)
    nout_copy = pltpu.make_async_copy(nout_v, nout_hbm, out_sem.at[0])
    nout_copy.start()
    draw = norm_backward(valid * ncot_v[...] * ngain[...], normed, inv).astype(BF)
    dpre = (mm_nt(draw, npout_v[...]) * act_slope(pre)).astype(BF)
    npart_v[...] = ncot_v[...] + mm_nt(dpre, npin_v[0:L, :])
    npart_copy = pltpu.make_async_copy(npart_v, npart_hbm, out_sem.at[1])
    npart_copy.start()
    dy_v[...] = mm_nt(dpre, npin_v[L:, :]).astype(BF)
    grad_in = mm_tn(nx_v[...], dpre).astype(BF)
    grad_out = mm_tn(hid, draw).astype(BF)
    for k in range(4):
        columns = slice(LANES * k, LANES * (k + 1))
        gnode_v[k, :, 0:64, :] = grad_in[:, columns].reshape(16, 64, LANES)
        gnode_v[k, :, 64:96, :] = grad_out[:, columns].reshape(16, 32, LANES)
    gnode_copy = pltpu.make_async_copy(gnode_v, gnode_hbm, out_sem.at[2])
    gnode_copy.start()

    def backward(i, carry):
        cot_load(i).wait()
        total = cot_v[rows(i), :] + mm(x_v[rows(i), HPAD:], dy_v[...])
        draw = norm_backward(total * gain[...], n_v[rows(i), :], inv_v[rows(i), :]).astype(BF)
        draw_v[rows(i), :] = draw
        put(i, draw_v, draw_hbm, draw_sem).start()
        dpre = (mm_nt(draw, pout_v[...]) * act_slope(pre_v[rows(i), :])).astype(BF)
        dpre_v[rows(i), :] = dpre
        put(i, dpre_v, dpre_hbm, dpre_sem).start()
        cot_v[rows(i), :] = total + mm_nt(dpre, pe_v[...])
        put(i, cot_v, egrad_hbm, egrad_sem).start()
        return carry

    lax.fori_loop(0, CHUNKS, backward, 0)
    nout_copy.wait()
    npart_copy.wait()
    gnode_copy.wait()
    for i in range(CHUNKS):
        put(i, enew_v, eout_hbm, eout_sem).wait()
        put(i, hid_v, hid_hbm, hid_sem).wait()
        put(i, draw_v, draw_hbm, draw_sem).wait()
        put(i, dpre_v, dpre_hbm, dpre_sem).wait()
        put(i, cot_v, egrad_hbm, egrad_sem).wait()


def run_rows(n_dom, *operands):
    hbm = pl.BlockSpec(memory_space=pl.ANY)
    vmem = pl.BlockSpec(memory_space=pltpu.VMEM)
    smem = pl.BlockSpec(memory_space=pltpu.SMEM)
    shape = jax.ShapeDtypeStruct
    dma = pltpu.SemaphoreType.DMA
    return pl.pallas_call(
        functools.partial(rows_kernel, n_dom),
        out_shape=[
            shape((N, L), BF),
            shape((E, L), BF),
            shape((E, L), F32),
            shape((E, L), BF),
            shape((E, L), BF),
            shape((E, L), BF),
            shape((4, 16, 96, LANES), BF),
            shape((N, L), F32),
        ],
        in_specs=[vmem, vmem, smem, vmem, hbm, hbm, hbm, hbm, hbm, vmem, vmem]
        + [hbm, vmem, hbm, vmem, vmem, hbm, hbm],
        out_specs=[hbm] * 8,
        scratch_shapes=[
            pltpu.VMEM((16, 128), I32),
            pltpu.VMEM((E, HPAD + N), BF),
            pltpu.VMEM((N, E), BF),
            pltpu.VMEM((E, L), BF),
            pltpu.VMEM((E, L), BF),
            pltpu.VMEM((N, L), BF),
            pltpu.VMEM((L, L), BF),
            pltpu.VMEM((L, L), BF),
            pltpu.VMEM((2 * L, L), BF),
            pltpu.VMEM((L, L), BF),
            pltpu.VMEM((N, L), F32),
            pltpu.VMEM((E, L), F32),
            pltpu.VMEM((E, L), F32),
            pltpu.VMEM((E, L), BF),
            pltpu.VMEM((E, L), F32),
            pltpu.VMEM((E, 1), F32),
            pltpu.VMEM((E, L), BF),
            pltpu.VMEM((E, L), BF),
            pltpu.VMEM((E, L), BF),
            pltpu.VMEM((N, 2 * L), BF),
            pltpu.VMEM((N, L), BF),
            pltpu.VMEM((N, L), BF),
            pltpu.VMEM((N, L), F32),
            pltpu.VMEM((4, 16, 96, LANES), BF),
            dma((6,)),
            dma((CHUNKS,)),
            dma((CHUNKS,)),
            dma((CHUNKS,)),
            dma((CHUNKS,)),
            dma((CHUNKS,)),
            dma((CHUNKS,)),
            dma((CHUNKS,)),
            dma((CHUNKS,)),
            dma((3,)),
        ],
        compiler_params=pltpu.CompilerParams(vmem_limit_bytes=VMEM_LIMIT),
        name="rows",
    )(*operands)


class Wave:
    def __init__(self, coords, refs):
        self.coords = coords
        (self.own, self.from_core, self.a1, self.b1, self.sa, self.sb, self.a2, self.b2) = refs[:8]
        self.send, self.recv = refs[8:]
        self.copies = []

    def start(self, src, dst, device):
        k = len(self.copies)
        copy = pltpu.make_async_remote_copy(
            src_ref=src,
            dst_ref=dst,
            send_sem=self.send.at[k],
            recv_sem=self.recv.at[k],
            device_id=(device,),
            device_id_type=MESH,
        )
        copy.start()
        self.copies.append(copy)

    def to_core(self, src, into=None):
        z, x, y, c = self.coords
        self.start(src, self.from_core if into is None else into, device_at(z, x, y, 1 - c))

    def first(self):
        z, x, y, c = self.coords
        self.copies[0].wait_recv()
        own, got = self.own, self.from_core
        for zz in range(4):
            own[0, zz] = (own[0, zz].astype(F32) + got[0, zz].astype(F32)).astype(BF)
        for o in (2, 1, 3):
            zp = lax.rem(z + 4 - o, 4)
            self.start(own.at[0, zp], self.a1.at[o - 1], device_at(zp, x, y, c))
        for zz in range(4):
            own[1, zz] = (own[1, zz].astype(F32) + got[1, zz].astype(F32)).astype(BF)
        for o in (2, 1, 3):
            xp = lax.rem(x + 4 - o, 4)
            self.start(own.at[1, :, xp], self.b1.at[o - 1], device_at(z, xp, y, c))

    def second(self):
        z, x, y, c = self.coords
        for copy in self.copies[1:4]:
            copy.wait_recv()
        a = self.own[0, z].astype(F32)
        for o in range(3):
            a = a + self.a1[o].astype(F32)
        self.sa[...] = a.astype(BF)
        for o in (2, 1, 3):
            xp = lax.rem(x + 4 - o, 4)
            self.start(self.sa.at[xp], self.a2.at[o - 1], device_at(z, xp, y, c))
        for copy in self.copies[4:7]:
            copy.wait_recv()
        b = self.own[1, :, x].astype(F32)
        for o in range(3):
            b = b + self.b1[o].astype(F32)
        self.sb[...] = b.astype(BF)
        for o in (2, 1, 3):
            zp = lax.rem(z + 4 - o, 4)
            self.start(self.sb.at[zp], self.b2.at[o - 1], device_at(zp, x, y, c))

    def third(self, block, at):
        z, x, y, c = self.coords
        for copy in self.copies[7:13]:
            copy.wait_recv()
        a, b = self.sa[x].astype(F32), self.sb[z].astype(F32)
        for o in range(3):
            a = a + self.a2[o].astype(F32)
            b = b + self.b2[o].astype(F32)
        block[at, 0:LANES] = a.astype(BF)
        block[at, LANES:WIDE] = b.astype(BF)

    def finish(self):
        for copy in self.copies:
            copy.wait_send()


def device_at(z, x, y, c):
    return ((z * 4 + x) * 4 + y) * 2 + c


def wave_scratch(depth):
    dma = pltpu.SemaphoreType.DMA
    return [
        pltpu.VMEM((2, 4, 4, depth, LANES), BF),
        pltpu.VMEM((2, 4, 4, depth, LANES), BF),
        pltpu.VMEM((3, 4, depth, LANES), BF),
        pltpu.VMEM((3, 4, depth, LANES), BF),
        pltpu.VMEM((4, depth, LANES), BF),
        pltpu.VMEM((4, depth, LANES), BF),
        pltpu.VMEM((3, depth, LANES), BF),
        pltpu.VMEM((3, depth, LANES), BF),
        dma((13,)),
        dma((13,)),
    ]


def sums_kernel(
    n_dom,
    snd_ref, rcv_ref, gnode_hbm, h_hbm, halo_hbm, e_hbm, pin_hbm, hid_hbm, draw_hbm, dpre_hbm,
    out_ref, part_ref, ret_ref,
    tab_v, e_v, hid_v, draw_v, dpre_v, ps_v, pr_v, st_v, rt_v, as_v, ar_v, there_in, there_out, y_v,
    block, sorted_v, got, in_sem, y_send, y_recv, last_send, last_recv,
    *wave_refs,
):
    me = lax.axis_index("dom")
    c = lax.rem(me, 2)
    y = lax.rem(me // 2, 4)
    x = lax.rem(me // 8, 4)
    z = me // 32
    m = lax.rem(me, 8)
    coords = (z, x, y, c)
    node_wave = Wave(coords, wave_refs[0:10])
    in_wave = Wave(coords, wave_refs[10:20])
    out_wave = Wave(coords, wave_refs[20:30])

    mine = pl.ds(pl.multiple_of(c * WIDE, WIDE), WIDE)
    theirs = pl.ds(pl.multiple_of((1 - c) * WIDE, WIDE), WIDE)
    halves = (theirs, mine)

    loads = []

    def load(src, dst):
        copy = pltpu.make_async_copy(src, dst, in_sem.at[len(loads)])
        copy.start()
        loads.append(copy)

    load(dpre_hbm.at[:, theirs], dpre_v.at[0])
    load(h_hbm, tab_v.at[pl.ds(0, N)])
    load(halo_hbm, tab_v.at[pl.ds(N, HPAD)])
    load(e_hbm, e_v)
    for lanes in range(2):
        for k in range(4):
            load(gnode_hbm.at[2 * c + lanes, pl.ds(4 * k, 4)], node_wave.own.at[lanes, k])
    load(dpre_hbm.at[:, mine], dpre_v.at[1])
    load(hid_hbm, hid_v)
    load(draw_hbm.at[:, theirs], draw_v.at[0])
    load(draw_hbm.at[:, mine], draw_v.at[1])
    for half in range(2):
        load(pin_hbm.at[pl.ds(L, L), halves[half]], ps_v.at[half])
        load(pin_hbm.at[pl.ds(2 * L, L), halves[half]], pr_v.at[half])

    owners = [lax.rem(me + slot_shift(s) + n_dom, n_dom) for s in range(SLOTS)]
    others = [device_at(z, x, 0, 0) + lax.rem(m + 8 - o, 8) for o in range(1, 8)]
    along = [device_at(lax.rem(z + o, 4), x, y, c) for o in range(1, 4)]
    along += [device_at(z, lax.rem(x + o, 4), y, c) for o in range(1, 4)]
    greet(owners + others + along)

    node_wave.to_core(gnode_hbm.at[pl.ds(2 * (1 - c), 2)], node_wave.from_core.reshape(2, 16, 96, LANES))

    index = table_index(snd_ref[...], me, n_dom)
    high = lax.broadcasted_iota(I32, (TAB, 128), 0)
    for k in range(E // 128):
        at = pl.ds(k * 128, 128)
        st_v[:, at] = (jnp.broadcast_to(index[k : k + 1, :], (TAB, 128)) == high).astype(F32).astype(BF)
        rt_v[:, at] = (
            (jnp.broadcast_to(rcv_ref[k : k + 1, :], (N, 128)) == high[0:N, :]).astype(F32).astype(BF)
        )

    def put_lanes(product, dst, depth):
        for lanes in range(2):
            part = product[:, LANES * lanes : LANES * (lanes + 1)]
            dst[lanes] = part.astype(BF).reshape(4, 4, depth, LANES)

    def in_products(half, dst):
        dpre = dpre_v[half]
        sent = mm(st_v[...], dpre).astype(BF)
        taken = mm(rt_v[...], dpre).astype(BF)
        as_v[half] = sent
        ar_v[half] = taken
        product = jnp.concatenate(
            [mm_tn(e_v[...], dpre), mm_tn(tab_v[...], sent), mm_tn(tab_v[0:N, :], taken)], axis=0
        )
        put_lanes(product, dst, 96)

    def out_products(half, dst):
        put_lanes(mm_tn(hid_v[...], draw_v[half]), dst, 32)

    for k in range(4):
        loads[k].wait()
    in_products(0, there_in)
    in_wave.to_core(there_in)
    for k in range(4, 12):
        loads[k].wait()
    node_wave.first()
    loads[12].wait()
    in_products(1, in_wave.own)
    in_wave.first()
    for k in range(13, 20):
        loads[k].wait()
    out_products(0, there_out)
    out_wave.to_core(there_out)
    node_wave.second()
    out_products(1, out_wave.own)
    out_wave.first()

    y_v[...] = mm_nt(as_v[0, N : N + HALO, :], ps_v[0]) + mm_nt(as_v[1, N : N + HALO, :], ps_v[1])
    returns = []
    for s in range(SLOTS):
        copy = pltpu.make_async_remote_copy(
            src_ref=y_v.at[pl.ds(s * HB, HB)],
            dst_ref=ret_ref.at[pl.ds(s * HB, HB)],
            send_sem=y_send.at[s],
            recv_sem=y_recv.at[s],
            device_id=(owners[s],),
            device_id_type=MESH,
        )
        copy.start()
        returns.append(copy)
    in_wave.second()
    part_ref[...] = (
        mm_nt(as_v[0, 0:N, :], ps_v[0])
        + mm_nt(as_v[1, 0:N, :], ps_v[1])
        + mm_nt(ar_v[0], pr_v[0])
        + mm_nt(ar_v[1], pr_v[1])
    ).astype(BF)
    node_wave.third(block, pl.ds(0, 96))
    out_wave.second()
    in_wave.third(block, pl.ds(96, 96))
    out_wave.third(block, pl.ds(192, 32))

    row = lax.broadcasted_iota(I32, (256, 224), 0)
    col = lax.broadcasted_iota(I32, (256, 224), 1)
    j = row // 32
    r = row - j * 32
    source = jnp.where(
        r < 8,
        8 * j + r,
        jnp.where(
            r < 12,
            64 + 4 * j + (r - 8),
            jnp.where(r < 24, 96 + 12 * j + (r - 12), jnp.where(r < 28, 192 + 4 * j + (r - 24), -1)),
        ),
    )
    order = (source == col).astype(F32).astype(BF)
    sorted_v[...] = mm(order, block[...]).astype(BF).reshape(8, 32, WIDE)
    lasts = []
    for o in range(1, 8):
        target = lax.rem(m + 8 - o, 8)
        copy = pltpu.make_async_remote_copy(
            src_ref=sorted_v.at[target],
            dst_ref=got.at[o - 1],
            send_sem=last_send.at[o - 1],
            recv_sem=last_recv.at[o - 1],
            device_id=(others[o - 1],),
            device_id_type=MESH,
        )
        copy.start()
        lasts.append(copy)
    for copy in lasts:
        copy.wait_recv()
    same = sorted_v[m].astype(F32)
    for o in (2, 4, 6):
        same = same + got[o - 1].astype(F32)
    cross = got[0].astype(F32)
    for o in (3, 5, 7):
        cross = cross + got[o - 1].astype(F32)
    even = c == 0
    out_ref[:, 0:WIDE] = jnp.where(even, same, cross)
    out_ref[:, WIDE:] = jnp.where(even, cross, same)
    for copy in returns:
        copy.wait()
    for copy in lasts:
        copy.wait_send()
    for wave in (node_wave, in_wave, out_wave):
        wave.finish()


def run_sums(n_dom, *operands):
    hbm = pl.BlockSpec(memory_space=pl.ANY)
    vmem = pl.BlockSpec(memory_space=pltpu.VMEM)
    shape = jax.ShapeDtypeStruct
    dma = pltpu.SemaphoreType.DMA
    return pl.pallas_call(
        functools.partial(sums_kernel, n_dom),
        out_shape=[shape((32, L), F32), shape((N, L), BF), shape((HALO, L), F32)],
        in_specs=[vmem, vmem] + [hbm] * 8,
        out_specs=[vmem, vmem, vmem],
        scratch_shapes=[
            pltpu.VMEM((TAB, L), BF),
            pltpu.VMEM((E, L), BF),
            pltpu.VMEM((E, L), BF),
            pltpu.VMEM((2, E, WIDE), BF),
            pltpu.VMEM((2, E, WIDE), BF),
            pltpu.VMEM((2, L, WIDE), BF),
            pltpu.VMEM((2, L, WIDE), BF),
            pltpu.VMEM((TAB, E), BF),
            pltpu.VMEM((N, E), BF),
            pltpu.VMEM((2, TAB, WIDE), BF),
            pltpu.VMEM((2, N, WIDE), BF),
            pltpu.VMEM((2, 4, 4, 96, LANES), BF),
            pltpu.VMEM((2, 4, 4, 32, LANES), BF),
            pltpu.VMEM((HALO, L), F32),
            pltpu.VMEM((224, WIDE), BF),
            pltpu.VMEM((8, 32, WIDE), BF),
            pltpu.VMEM((7, 32, WIDE), BF),
            dma((20,)),
            dma((SLOTS,)),
            dma((SLOTS,)),
            dma((7,)),
            dma((7,)),
        ]
        + wave_scratch(96)
        + wave_scratch(96)
        + wave_scratch(32),
        compiler_params=pltpu.CompilerParams(
            collective_id=1, has_side_effects=True, vmem_limit_bytes=VMEM_LIMIT
        ),
        name="sums",
    )(*operands)


def last_kernel(
    n_dom, edge_factor, node_factor,
    rows_ref, sums_ref, part_ref, ret_ref, npart_ref,
    grad_ref, ein_ref, eout_ref, nin_ref, nout_ref,
):
    me = lax.axis_index("dom")
    grad_ref[...] = npart_ref[...] + part_ref[...].astype(F32)
    for s in range(SLOTS):
        reader = lax.rem(me - slot_shift(s) + n_dom, n_dom)
        for k in range(HB):
            at = pl.ds(rows_ref[k, reader], 1)
            grad_ref[at, :] = grad_ref[at, :] + ret_ref[s * HB + k : s * HB + k + 1, :]
    nin_ref[0] = sums_ref[0:8, :] * node_factor
    nout_ref[0] = sums_ref[8:12, :] * node_factor
    ein_ref[...] = (sums_ref[12:24, :] * edge_factor).reshape(12, 1, L)
    eout_ref[0] = sums_ref[24:28, :] * edge_factor


def run_last(n_dom, edge_factor, node_factor, *operands):
    vmem = pl.BlockSpec(memory_space=pltpu.VMEM)
    smem = pl.BlockSpec(memory_space=pltpu.SMEM)
    shape = jax.ShapeDtypeStruct
    return pl.pallas_call(
        functools.partial(last_kernel, n_dom, edge_factor, node_factor),
        out_shape=[
            shape((N, L), F32),
            shape((12, 1, L), F32),
            shape((1, 4, L), F32),
            shape((1, 8, L), F32),
            shape((1, 4, L), F32),
        ],
        in_specs=[smem, vmem, vmem, vmem, vmem],
        out_specs=[vmem] * 5,
        name="last",
    )(*operands)


def per_device(
    node_latent,
    edge_latent,
    sender_index,
    receiver_index,
    send_rows,
    node_count,
    edge_proj_in,
    edge_bias_in,
    edge_proj_out,
    edge_bias_out,
    edge_gain,
    node_proj_in,
    node_bias_in,
    node_proj_out,
    node_bias_out,
    node_gain,
    node_cot,
    edge_cot,
):
    n_dom = lax.axis_size("dom")
    slot_rows = send_rows.transpose(0, 2, 1).reshape(HB, n_dom)
    snd = sender_index.reshape(E // 128, 128)
    rcv = receiver_index.reshape(E // 128, 128)
    pin, pout = edge_proj_in.reshape(3 * L, L), edge_proj_out.reshape(L, L)
    halo, thalo, pre_part = run_halo(
        n_dom, snd, rcv, slot_rows, node_latent, edge_latent, pin, edge_bias_in
    )
    node_out, edge_out, edge_grad, dpre, draw, hid, gnode, npart = run_rows(
        n_dom, snd, rcv, node_count, thalo, node_latent, pre_part, edge_latent, pin, pout,
        edge_bias_out, edge_gain, node_proj_in.reshape(2 * L, L), node_bias_in,
        node_proj_out.reshape(L, L), node_bias_out, node_gain, node_cot, edge_cot,
    )
    sums, part, returned = run_sums(
        n_dom, snd, rcv, gnode, node_latent, halo, edge_latent, pin, hid, draw, dpre
    )
    edge_factor = float(E * n_dom) ** (-0.5)
    node_factor = float(N * n_dom) ** (-0.5)
    node_grad, edge_in, edge_out_grad, node_in, node_out_grad = run_last(
        n_dom, edge_factor, node_factor, slot_rows, sums, part, returned, npart
    )
    edge_in = edge_in.transpose(1, 0, 2)
    return node_out, edge_out, node_grad, edge_grad, edge_in, edge_out_grad, node_in, node_out_grad


def solution(mesh):
    rows = P("dom", None)
    one = P("dom")
    whole = P()
    in_specs = (rows, rows, one, one, P("dom", None, None), one) + (whole,) * 10 + (rows, rows)
    split = P(None, "dom", None)
    out_specs = (rows,) * 4 + (split,) * 4
    return jax.shard_map(per_device, mesh=mesh, in_specs=in_specs, out_specs=out_specs, check_vma=False)
```

```python
import functools

import jax
import jax.numpy as jnp
from jax import lax
from jax.experimental import pallas as pl
from jax.experimental.pallas import tpu as pltpu
from jax.sharding import PartitionSpec as P

EPS = 1e-05
MESH = pl.DeviceIdType.MESH
BF = jnp.bfloat16
F32 = jnp.float32
I32 = jnp.int32

L = 512
N = 512
E = 2048
HB = 8
SLOTS = 9
HALO = SLOTS * HB
HPAD = 128
TAB = N + HPAD
C = 512
CHUNKS = E // C
S = 256
WIDE = L // 2
LANES = 128
VMEM_LIMIT = 56 * 1024 * 1024

NT = (((1,), (1,)), ((), ()))
TN = (((0,), (0,)), ((), ()))


def slot_shift(slot):
    return 64 if slot == 4 else slot - 4


def mm(a, b):
    return jnp.dot(a, b, preferred_element_type=F32)


def mm_nt(a, b):
    return lax.dot_general(a, b, NT, preferred_element_type=F32)


def mm_tn(a, b):
    return lax.dot_general(a, b, TN, preferred_element_type=F32)


def staggered(*streams):
    live = list(streams)
    turn = 0
    while live:
        for stream in live[: turn + 1]:
            if next(stream, StopIteration) is StopIteration:
                live.remove(stream)
                turn -= 1
        turn += 1


def sigmoid(x):
    return 0.5 * jnp.tanh(0.5 * x) + 0.5


def table_index(sender, me, n_dom):
    far = sender - N
    peer = far // HB
    row = far - peer * HB
    turn = lax.rem(peer - me + (n_dom + 4), n_dom)
    slot = jnp.where(turn == 68, 4, turn)
    return jnp.where(sender < N, sender, N + slot * HB + row)


def boundary_rows(rows_ref, readers):
    lane = lax.broadcasted_iota(I32, (HB, 128), 1)
    node = lax.broadcasted_iota(I32, (HB, N), 1)
    listed = rows_ref[...]
    picked = []
    for reader in readers:
        column = jnp.sum(jnp.where(lane == reader, listed, 0), axis=1, keepdims=True)
        picked.append((jnp.broadcast_to(column, (HB, N)) == node).astype(F32))
    return jnp.concatenate(picked, axis=0).astype(BF)


def greet(devices):
    barrier = pltpu.get_barrier_semaphore()
    for device in devices:
        pl.semaphore_signal(barrier, inc=1, device_id=(device,), device_id_type=MESH)
    pl.semaphore_wait(barrier, len(devices))


def one_hot_columns(index, lane, blocks):
    column = jnp.broadcast_to(index, (128, 128)).T
    return jnp.concatenate(
        [(column == lane + 128 * m).astype(F32).astype(BF) for m in range(blocks)], axis=1
    )


def halo_kernel(
    n_dom,
    snd_ref, rcv_ref, rows_ref, h_hbm, e_hbm, pin_hbm, b_in,
    halo_ref, thalo_ref, pre_hbm,
    h_v, x_v, pin_v, t_v, pre_v, outgoing, incoming,
    in_sem, e_sem, pre_sem, send_sem, recv_sem,
):
    me = lax.axis_index("dom")
    targets = [lax.rem(me - slot_shift(s) + n_dom, n_dom) for s in range(SLOTS)]

    def rows(i):
        return pl.ds(pl.multiple_of(i * C, C), C)

    def e_load(i):
        return pltpu.make_async_copy(e_hbm.at[rows(i)], x_v.at[rows(i), pl.ds(0, L)], e_sem.at[i])

    def pre_put(i):
        return pltpu.make_async_copy(pre_v.at[rows(i)], pre_hbm.at[rows(i)], pre_sem.at[i])

    barrier = pltpu.get_barrier_semaphore()
    for device in targets:
        pl.semaphore_signal(barrier, inc=1, device_id=(device,), device_id_type=MESH)
    h_load = pltpu.make_async_copy(h_hbm, h_v, in_sem.at[0])
    h_load.start()
    pin_load = pltpu.make_async_copy(pin_hbm, pin_v, in_sem.at[1])
    pin_load.start()
    for i in range(CHUNKS):
        e_load(i).start()
    h_load.wait()
    outgoing[...] = mm(boundary_rows(rows_ref, targets), h_v[...])
    pl.semaphore_wait(barrier, SLOTS)
    copies = []
    for s in range(SLOTS):
        copy = pltpu.make_async_remote_copy(
            src_ref=outgoing.at[pl.ds(s * HB, HB)],
            dst_ref=incoming.at[pl.ds(s * HB, HB)],
            send_sem=send_sem.at[s],
            recv_sem=recv_sem.at[s],
            device_id=(targets[s],),
            device_id_type=MESH,
        )
        copy.start()
        copies.append(copy)

    pin_load.wait()
    t_v[0:L, :] = pin_v[0:L, :]
    t_v[L : 2 * L, :] = mm(h_v[...], pin_v[L : 2 * L, :]).astype(BF)
    t_v[2 * L :, :] = (mm(h_v[...], pin_v[2 * L :, :]) + b_in[...]).astype(BF)
    lane = lax.broadcasted_iota(I32, (128, 128), 1)

    def local(i, carry):
        for b in range(C // 128):
            block = i * (C // 128) + b
            at = pl.ds(pl.multiple_of(block * 128, 128), 128)
            x_v[at, L : 2 * L] = one_hot_columns(snd_ref[pl.ds(block, 1), :], lane, N // 128)
            x_v[at, 2 * L :] = one_hot_columns(rcv_ref[pl.ds(block, 1), :], lane, N // 128)
        e_load(i).wait()
        pre_v[rows(i), :] = mm(x_v[rows(i), :], t_v[...]).astype(BF)
        pre_put(i).start()
        return carry

    lax.fori_loop(0, CHUNKS, local, 0)
    for copy in copies:
        copy.wait()
    halo = jnp.concatenate([incoming[...].astype(BF), jnp.zeros((HPAD - HALO, L), BF)], axis=0)
    halo_ref[...] = halo
    thalo_ref[...] = mm(halo, pin_v[L : 2 * L, :]).astype(BF)
    for i in range(CHUNKS):
        pre_put(i).wait()


def run_halo(n_dom, *operands):
    hbm = pl.BlockSpec(memory_space=pl.ANY)
    vmem = pl.BlockSpec(memory_space=pltpu.VMEM)
    shape = jax.ShapeDtypeStruct
    dma = pltpu.SemaphoreType.DMA
    return pl.pallas_call(
        functools.partial(halo_kernel, n_dom),
        out_shape=[shape((HPAD, L), BF), shape((HPAD, L), BF), shape((E, L), BF)],
        in_specs=[vmem, vmem, vmem, hbm, hbm, hbm, vmem],
        out_specs=[vmem, vmem, hbm],
        scratch_shapes=[
            pltpu.VMEM((N, L), BF),
            pltpu.VMEM((E, 3 * L), BF),
            pltpu.VMEM((3 * L, L), BF),
            pltpu.VMEM((3 * L, L), BF),
            pltpu.VMEM((E, L), BF),
            pltpu.VMEM((HALO, L), F32),
            pltpu.VMEM((HALO, L), F32),
            dma((2,)),
            dma((CHUNKS,)),
            dma((CHUNKS,)),
            dma((SLOTS,)),
            dma((SLOTS,)),
        ],
        compiler_params=pltpu.CompilerParams(
            collective_id=0, has_side_effects=True, vmem_limit_bytes=VMEM_LIMIT
        ),
        name="halo",
    )(*operands)


def norm_forward(raw):
    centered = raw - jnp.mean(raw, axis=-1, keepdims=True)
    inv = lax.rsqrt(jnp.mean(centered * centered, axis=-1, keepdims=True) + EPS)
    return centered * inv, inv


def norm_backward(q, normed, inv):
    first = jnp.mean(q, axis=-1, keepdims=True)
    second = jnp.mean(q * normed, axis=-1, keepdims=True)
    return inv * (q - first - normed * second)


def act_slope(pre):
    gate = sigmoid(pre)
    return gate * (1.0 + pre * (1.0 - gate))


def rows_kernel(
    n_dom,
    snd_ref, rcv_ref, cnt_ref, thalo_ref, h_hbm, part_hbm, e_hbm, pin_hbm, pout_hbm, b_out, gain,
    npin_hbm, nb_in, npout_hbm, nb_out, ngain, ncot_hbm, ecot_hbm,
    nout_hbm, eout_hbm, egrad_hbm, dpre_hbm, draw_hbm, hid_hbm, gnode_hbm, npart_hbm,
    idx_v, x_v, rt_v, e_v, part_v, h_v, pe_v, pout_v, npin_v, npout_v, ncot_v, cot_v,
    pre_v, hid_v, n_v, inv_v, enew_v, draw_v, dpre_v, nx_v, dy_v, nout_v, npart_v, gnode_v,
    in_sem, e_sem, part_sem, cot_sem, eout_sem, hid_sem, draw_sem, dpre_sem, egrad_sem, out_sem,
):
    me = lax.axis_index("dom")

    def load(k, src, dst):
        return pltpu.make_async_copy(src, dst, in_sem.at[k])

    def rows(i):
        return pl.ds(pl.multiple_of(i * C, C), C)

    def e_load(i):
        return pltpu.make_async_copy(e_hbm.at[rows(i)], e_v.at[rows(i)], e_sem.at[i])

    def part_load(i):
        return pltpu.make_async_copy(part_hbm.at[rows(i)], part_v.at[rows(i)], part_sem.at[i])

    def cot_load(i):
        return pltpu.make_async_copy(ecot_hbm.at[rows(i)], cot_v.at[rows(i)], cot_sem.at[i])

    def put(i, src, dst, sem):
        return pltpu.make_async_copy(src.at[rows(i)], dst.at[rows(i)], sem.at[i])

    loads = [
        load(0, pout_hbm, pout_v),
        load(1, h_hbm, h_v),
        load(2, npin_hbm, npin_v),
        load(3, npout_hbm, npout_v),
        load(4, ncot_hbm, ncot_v),
        load(5, pin_hbm.at[pl.ds(0, L)], pe_v),
    ]
    part_load(0).start()
    loads[0].start()
    for i in range(CHUNKS):
        e_load(i).start()
        if i + 1 < CHUNKS:
            part_load(i + 1).start()
    for k in range(1, 6):
        loads[k].start()
    for i in range(CHUNKS):
        cot_load(i).start()

    idx_v[...] = table_index(snd_ref[...], me, n_dom)
    lane = lax.broadcasted_iota(I32, (128, 128), 1)
    high = lax.broadcasted_iota(I32, (N, 128), 0)
    loads[0].wait()

    def forward_rows(first):
        for b in range(S // 128):
            at = pl.ds(pl.multiple_of(first + b * 128, 128), 128)
            block = first // 128 + b
            r_row = rcv_ref[pl.ds(block, 1), :]
            x_v[at, 0:HPAD] = one_hot_columns(idx_v[pl.ds(block, 1), :] - N, lane, 1)
            x_v[at, HPAD:] = one_hot_columns(r_row, lane, N // 128)
            rt_v[:, at] = (jnp.broadcast_to(r_row, (N, 128)) == high).astype(F32).astype(BF)
        at = pl.ds(pl.multiple_of(first, S), S)
        pre = part_v[at, :].astype(F32) + mm(x_v[at, 0:HPAD], thalo_ref[...])
        yield
        pre_v[at, :] = pre
        hid = (pre * sigmoid(pre)).astype(BF)
        hid_v[at, :] = hid
        yield
        raw = mm(hid, pout_v[...]) + b_out[...]
        yield
        normed, inv = norm_forward(raw)
        n_v[at, :] = normed
        inv_v[at, :] = inv
        enew_v[at, :] = (e_v[at, :].astype(F32) + normed * gain[...]).astype(BF)

    def forward(i, carry):
        part_load(i).wait()
        e_load(i).wait()
        staggered(*[forward_rows(i * C + s * S) for s in range(C // S)])
        put(i, enew_v, eout_hbm, eout_sem).start()
        put(i, hid_v, hid_hbm, hid_sem).start()
        return carry

    lax.fori_loop(0, CHUNKS, forward, 0)

    valid = (lax.broadcasted_iota(I32, (N, 1), 0) < cnt_ref[0]).astype(F32)
    nx_v[:, L:] = (mm(rt_v[...], enew_v[...]) * valid).astype(BF)
    for k in range(1, 6):
        loads[k].wait()
    nx_v[:, 0:L] = h_v[...]
    pre = mm(nx_v[...], npin_v[...]) + nb_in[...]
    hid = (pre * sigmoid(pre)).astype(BF)
    normed, inv = norm_forward(mm(hid, npout_v[...]) + nb_out[...])
    nout_v[...] = (h_v[...].astype(F32) + valid * (normed * ngain[...])).astype(BF)
    nout_copy = pltpu.make_async_copy(nout_v, nout_hbm, out_sem.at[0])
    nout_copy.start()
    draw = norm_backward(valid * ncot_v[...] * ngain[...], normed, inv).astype(BF)
    dpre = (mm_nt(draw, npout_v[...]) * act_slope(pre)).astype(BF)
    npart_v[...] = ncot_v[...] + mm_nt(dpre, npin_v[0:L, :])
    npart_copy = pltpu.make_async_copy(npart_v, npart_hbm, out_sem.at[1])
    npart_copy.start()
    dy_v[...] = mm_nt(dpre, npin_v[L:, :]).astype(BF)
    grad_in = mm_tn(nx_v[...], dpre).astype(BF)
    grad_out = mm_tn(hid, draw).astype(BF)
    for k in range(4):
        columns = slice(LANES * k, LANES * (k + 1))
        gnode_v[k, :, 0:64, :] = grad_in[:, columns].reshape(16, 64, LANES)
        gnode_v[k, :, 64:96, :] = grad_out[:, columns].reshape(16, 32, LANES)
    gnode_copy = pltpu.make_async_copy(gnode_v, gnode_hbm, out_sem.at[2])
    gnode_copy.start()

    def backward_rows(first):
        at = pl.ds(pl.multiple_of(first, S), S)
        total = cot_v[at, :] + mm(x_v[at, HPAD:], dy_v[...])
        yield
        draw = norm_backward(total * gain[...], n_v[at, :], inv_v[at, :]).astype(BF)
        draw_v[at, :] = draw
        yield
        dhid = mm_nt(draw, pout_v[...])
        yield
        dpre = (dhid * act_slope(pre_v[at, :])).astype(BF)
        dpre_v[at, :] = dpre
        yield
        cot_v[at, :] = total + mm_nt(dpre, pe_v[...])

    def backward(i, carry):
        cot_load(i).wait()
        staggered(*[backward_rows(i * C + s * S) for s in range(C // S)])
        put(i, draw_v, draw_hbm, draw_sem).start()
        put(i, dpre_v, dpre_hbm, dpre_sem).start()
        put(i, cot_v, egrad_hbm, egrad_sem).start()
        return carry

    lax.fori_loop(0, CHUNKS, backward, 0)
    nout_copy.wait()
    npart_copy.wait()
    gnode_copy.wait()
    for i in range(CHUNKS):
        put(i, enew_v, eout_hbm, eout_sem).wait()
        put(i, hid_v, hid_hbm, hid_sem).wait()
        put(i, draw_v, draw_hbm, draw_sem).wait()
        put(i, dpre_v, dpre_hbm, dpre_sem).wait()
        put(i, cot_v, egrad_hbm, egrad_sem).wait()


def run_rows(n_dom, *operands):
    hbm = pl.BlockSpec(memory_space=pl.ANY)
    vmem = pl.BlockSpec(memory_space=pltpu.VMEM)
    smem = pl.BlockSpec(memory_space=pltpu.SMEM)
    shape = jax.ShapeDtypeStruct
    dma = pltpu.SemaphoreType.DMA
    return pl.pallas_call(
        functools.partial(rows_kernel, n_dom),
        out_shape=[
            shape((N, L), BF),
            shape((E, L), BF),
            shape((E, L), F32),
            shape((E, L), BF),
            shape((E, L), BF),
            shape((E, L), BF),
            shape((4, 16, 96, LANES), BF),
            shape((N, L), F32),
        ],
        in_specs=[vmem, vmem, smem, vmem, hbm, hbm, hbm, hbm, hbm, vmem, vmem]
        + [hbm, vmem, hbm, vmem, vmem, hbm, hbm],
        out_specs=[hbm] * 8,
        scratch_shapes=[
            pltpu.VMEM((16, 128), I32),
            pltpu.VMEM((E, HPAD + N), BF),
            pltpu.VMEM((N, E), BF),
            pltpu.VMEM((E, L), BF),
            pltpu.VMEM((E, L), BF),
            pltpu.VMEM((N, L), BF),
            pltpu.VMEM((L, L), BF),
            pltpu.VMEM((L, L), BF),
            pltpu.VMEM((2 * L, L), BF),
            pltpu.VMEM((L, L), BF),
            pltpu.VMEM((N, L), F32),
            pltpu.VMEM((E, L), F32),
            pltpu.VMEM((E, L), F32),
            pltpu.VMEM((E, L), BF),
            pltpu.VMEM((E, L), F32),
            pltpu.VMEM((E, 1), F32),
            pltpu.VMEM((E, L), BF),
            pltpu.VMEM((E, L), BF),
            pltpu.VMEM((E, L), BF),
            pltpu.VMEM((N, 2 * L), BF),
            pltpu.VMEM((N, L), BF),
            pltpu.VMEM((N, L), BF),
            pltpu.VMEM((N, L), F32),
            pltpu.VMEM((4, 16, 96, LANES), BF),
            dma((6,)),
            dma((CHUNKS,)),
            dma((CHUNKS,)),
            dma((CHUNKS,)),
            dma((CHUNKS,)),
            dma((CHUNKS,)),
            dma((CHUNKS,)),
            dma((CHUNKS,)),
            dma((CHUNKS,)),
            dma((3,)),
        ],
        compiler_params=pltpu.CompilerParams(vmem_limit_bytes=VMEM_LIMIT),
        name="rows",
    )(*operands)


class Wave:
    def __init__(self, coords, refs):
        self.coords = coords
        (self.own, self.from_core, self.a1, self.b1, self.sa, self.sb, self.a2, self.b2) = refs[:8]
        self.send, self.recv = refs[8:]
        self.copies = []

    def start(self, src, dst, device):
        k = len(self.copies)
        copy = pltpu.make_async_remote_copy(
            src_ref=src,
            dst_ref=dst,
            send_sem=self.send.at[k],
            recv_sem=self.recv.at[k],
            device_id=(device,),
            device_id_type=MESH,
        )
        copy.start()
        self.copies.append(copy)

    def to_core(self, src, into=None):
        z, x, y, c = self.coords
        self.start(src, self.from_core if into is None else into, device_at(z, x, y, 1 - c))

    def first(self):
        z, x, y, c = self.coords
        self.copies[0].wait_recv()
        own, got = self.own, self.from_core
        for zz in range(4):
            own[0, zz] = (own[0, zz].astype(F32) + got[0, zz].astype(F32)).astype(BF)
        for o in (2, 1, 3):
            zp = lax.rem(z + 4 - o, 4)
            self.start(own.at[0, zp], self.a1.at[o - 1], device_at(zp, x, y, c))
        for zz in range(4):
            own[1, zz] = (own[1, zz].astype(F32) + got[1, zz].astype(F32)).astype(BF)
        for o in (2, 1, 3):
            xp = lax.rem(x + 4 - o, 4)
            self.start(own.at[1, :, xp], self.b1.at[o - 1], device_at(z, xp, y, c))

    def second(self):
        z, x, y, c = self.coords
        for copy in self.copies[1:4]:
            copy.wait_recv()
        a = self.own[0, z].astype(F32)
        for o in range(3):
            a = a + self.a1[o].astype(F32)
        self.sa[...] = a.astype(BF)
        for o in (2, 1, 3):
            xp = lax.rem(x + 4 - o, 4)
            self.start(self.sa.at[xp], self.a2.at[o - 1], device_at(z, xp, y, c))
        for copy in self.copies[4:7]:
            copy.wait_recv()
        b = self.own[1, :, x].astype(F32)
        for o in range(3):
            b = b + self.b1[o].astype(F32)
        self.sb[...] = b.astype(BF)
        for o in (2, 1, 3):
            zp = lax.rem(z + 4 - o, 4)
            self.start(self.sb.at[zp], self.b2.at[o - 1], device_at(zp, x, y, c))

    def third(self, block, at):
        z, x, y, c = self.coords
        for copy in self.copies[7:13]:
            copy.wait_recv()
        a, b = self.sa[x].astype(F32), self.sb[z].astype(F32)
        for o in range(3):
            a = a + self.a2[o].astype(F32)
            b = b + self.b2[o].astype(F32)
        block[at, 0:LANES] = a.astype(BF)
        block[at, LANES:WIDE] = b.astype(BF)

    def finish(self):
        for copy in self.copies:
            copy.wait_send()


def device_at(z, x, y, c):
    return ((z * 4 + x) * 4 + y) * 2 + c


def wave_scratch(depth):
    dma = pltpu.SemaphoreType.DMA
    return [
        pltpu.VMEM((2, 4, 4, depth, LANES), BF),
        pltpu.VMEM((2, 4, 4, depth, LANES), BF),
        pltpu.VMEM((3, 4, depth, LANES), BF),
        pltpu.VMEM((3, 4, depth, LANES), BF),
        pltpu.VMEM((4, depth, LANES), BF),
        pltpu.VMEM((4, depth, LANES), BF),
        pltpu.VMEM((3, depth, LANES), BF),
        pltpu.VMEM((3, depth, LANES), BF),
        dma((13,)),
        dma((13,)),
    ]


def sums_kernel(
    n_dom,
    snd_ref, rcv_ref, rows_ref, gnode_hbm, h_hbm, halo_hbm, e_hbm, pin_hbm, hid_hbm, draw_hbm, dpre_hbm,
    out_ref, part_ref,
    tab_v, e_v, hid_v, draw_v, dpre_v, ps_v, pr_v, st_v, rt_v, as_v, ar_v, there_in, there_out, y_v, ret_ref, part_v,
    block, sorted_v, got, in_sem, y_send, y_recv, last_send, last_recv,
    *wave_refs,
):
    me = lax.axis_index("dom")
    c = lax.rem(me, 2)
    y = lax.rem(me // 2, 4)
    x = lax.rem(me // 8, 4)
    z = me // 32
    m = lax.rem(me, 8)
    coords = (z, x, y, c)
    node_wave = Wave(coords, wave_refs[0:10])
    in_wave = Wave(coords, wave_refs[10:20])
    out_wave = Wave(coords, wave_refs[20:30])

    mine = pl.ds(pl.multiple_of(c * WIDE, WIDE), WIDE)
    theirs = pl.ds(pl.multiple_of((1 - c) * WIDE, WIDE), WIDE)
    halves = (theirs, mine)

    loads = []

    def load(src, dst):
        copy = pltpu.make_async_copy(src, dst, in_sem.at[len(loads)])
        copy.start()
        loads.append(copy)

    for lanes in range(2):
        for k in range(4):
            load(gnode_hbm.at[2 * c + lanes, pl.ds(4 * k, 4)], node_wave.own.at[lanes, k])
    load(dpre_hbm.at[:, theirs], dpre_v.at[0])
    load(e_hbm, e_v)
    load(h_hbm, tab_v.at[pl.ds(0, N)])
    load(halo_hbm, tab_v.at[pl.ds(N, HPAD)])
    load(dpre_hbm.at[:, mine], dpre_v.at[1])
    load(hid_hbm, hid_v)
    load(draw_hbm.at[:, theirs], draw_v.at[0])
    load(draw_hbm.at[:, mine], draw_v.at[1])
    for half in range(2):
        load(pin_hbm.at[pl.ds(L, L), halves[half]], ps_v.at[half])
        load(pin_hbm.at[pl.ds(2 * L, L), halves[half]], pr_v.at[half])

    owners = [lax.rem(me + slot_shift(s) + n_dom, n_dom) for s in range(SLOTS)]
    others = [device_at(z, x, 0, 0) + lax.rem(m + 8 - o, 8) for o in range(1, 8)]
    along = [device_at(lax.rem(z + o, 4), x, y, c) for o in range(1, 4)]
    along += [device_at(z, lax.rem(x + o, 4), y, c) for o in range(1, 4)]
    greet(owners + others + along)

    node_wave.to_core(gnode_hbm.at[pl.ds(2 * (1 - c), 2)], node_wave.from_core.reshape(2, 16, 96, LANES))

    index = table_index(snd_ref[...], me, n_dom)
    high = lax.broadcasted_iota(I32, (TAB, 128), 0)
    for k in range(E // 128):
        at = pl.ds(k * 128, 128)
        st_v[:, at] = (jnp.broadcast_to(index[k : k + 1, :], (TAB, 128)) == high).astype(F32).astype(BF)
        rt_v[:, at] = (
            (jnp.broadcast_to(rcv_ref[k : k + 1, :], (N, 128)) == high[0:N, :]).astype(F32).astype(BF)
        )

    def put_lanes(product, dst, depth):
        for lanes in range(2):
            part = product[:, LANES * lanes : LANES * (lanes + 1)]
            dst[lanes] = part.astype(BF).reshape(4, 4, depth, LANES)

    def in_products(half, dst):
        dpre = dpre_v[half]
        sent = mm(st_v[...], dpre).astype(BF)
        taken = mm(rt_v[...], dpre).astype(BF)
        as_v[half] = sent
        ar_v[half] = taken
        product = jnp.concatenate(
            [mm_tn(e_v[...], dpre), mm_tn(tab_v[...], sent), mm_tn(tab_v[0:N, :], taken)], axis=0
        )
        put_lanes(product, dst, 96)

    def out_products(half, dst):
        put_lanes(mm_tn(hid_v[...], draw_v[half]), dst, 32)

    for k in range(8):
        loads[k].wait()
    node_wave.first()
    for k in range(8, 12):
        loads[k].wait()
    in_products(0, there_in)
    in_wave.to_core(there_in)
    loads[12].wait()
    in_products(1, in_wave.own)
    in_wave.first()
    for k in range(13, 20):
        loads[k].wait()
    out_products(0, there_out)
    out_wave.to_core(there_out)
    node_wave.second()
    out_products(1, out_wave.own)
    out_wave.first()

    y_v[...] = mm_nt(as_v[0, N : N + HALO, :], ps_v[0]) + mm_nt(as_v[1, N : N + HALO, :], ps_v[1])
    returns = []
    for s in range(SLOTS):
        copy = pltpu.make_async_remote_copy(
            src_ref=y_v.at[pl.ds(s * HB, HB)],
            dst_ref=ret_ref.at[pl.ds(s * HB, HB)],
            send_sem=y_send.at[s],
            recv_sem=y_recv.at[s],
            device_id=(owners[s],),
            device_id_type=MESH,
        )
        copy.start()
        returns.append(copy)
    in_wave.second()
    part_v[...] = (
        mm_nt(as_v[0, 0:N, :], ps_v[0])
        + mm_nt(as_v[1, 0:N, :], ps_v[1])
        + mm_nt(ar_v[0], pr_v[0])
        + mm_nt(ar_v[1], pr_v[1])
    )
    out_wave.second()
    node_wave.third(block, pl.ds(0, 96))
    for copy in returns:
        copy.wait()
    readers = [lax.rem(me - slot_shift(s) + n_dom, n_dom) for s in range(SLOTS)]
    part_ref[...] = (part_v[...] + mm_tn(boundary_rows(rows_ref, readers), ret_ref[...].astype(BF))).astype(BF)
    in_wave.third(block, pl.ds(96, 96))
    out_wave.third(block, pl.ds(192, 32))

    row = lax.broadcasted_iota(I32, (256, 224), 0)
    col = lax.broadcasted_iota(I32, (256, 224), 1)
    j = row // 32
    r = row - j * 32
    source = jnp.where(
        r < 8,
        8 * j + r,
        jnp.where(
            r < 12,
            64 + 4 * j + (r - 8),
            jnp.where(r < 24, 96 + 12 * j + (r - 12), jnp.where(r < 28, 192 + 4 * j + (r - 24), -1)),
        ),
    )
    order = (source == col).astype(F32).astype(BF)
    sorted_v[...] = mm(order, block[...]).astype(BF).reshape(8, 32, WIDE)
    lasts = []
    for o in range(1, 8):
        target = lax.rem(m + 8 - o, 8)
        copy = pltpu.make_async_remote_copy(
            src_ref=sorted_v.at[target],
            dst_ref=got.at[o - 1],
            send_sem=last_send.at[o - 1],
            recv_sem=last_recv.at[o - 1],
            device_id=(others[o - 1],),
            device_id_type=MESH,
        )
        copy.start()
        lasts.append(copy)
    for copy in lasts:
        copy.wait_recv()
    same = sorted_v[m].astype(F32)
    for o in (2, 4, 6):
        same = same + got[o - 1].astype(F32)
    cross = got[0].astype(F32)
    for o in (3, 5, 7):
        cross = cross + got[o - 1].astype(F32)
    even = c == 0
    out_ref[:, 0:WIDE] = jnp.where(even, same, cross)
    out_ref[:, WIDE:] = jnp.where(even, cross, same)
    for copy in lasts:
        copy.wait_send()
    for wave in (node_wave, in_wave, out_wave):
        wave.finish()


def run_sums(n_dom, *operands):
    hbm = pl.BlockSpec(memory_space=pl.ANY)
    vmem = pl.BlockSpec(memory_space=pltpu.VMEM)
    shape = jax.ShapeDtypeStruct
    dma = pltpu.SemaphoreType.DMA
    return pl.pallas_call(
        functools.partial(sums_kernel, n_dom),
        out_shape=[shape((32, L), F32), shape((N, L), BF)],
        in_specs=[vmem, vmem, vmem] + [hbm] * 8,
        out_specs=[vmem, vmem],
        scratch_shapes=[
            pltpu.VMEM((TAB, L), BF),
            pltpu.VMEM((E, L), BF),
            pltpu.VMEM((E, L), BF),
            pltpu.VMEM((2, E, WIDE), BF),
            pltpu.VMEM((2, E, WIDE), BF),
            pltpu.VMEM((2, L, WIDE), BF),
            pltpu.VMEM((2, L, WIDE), BF),
            pltpu.VMEM((TAB, E), BF),
            pltpu.VMEM((N, E), BF),
            pltpu.VMEM((2, TAB, WIDE), BF),
            pltpu.VMEM((2, N, WIDE), BF),
            pltpu.VMEM((2, 4, 4, 96, LANES), BF),
            pltpu.VMEM((2, 4, 4, 32, LANES), BF),
            pltpu.VMEM((HALO, L), F32),
            pltpu.VMEM((HALO, L), F32),
            pltpu.VMEM((N, L), F32),
            pltpu.VMEM((224, WIDE), BF),
            pltpu.VMEM((8, 32, WIDE), BF),
            pltpu.VMEM((7, 32, WIDE), BF),
            dma((20,)),
            dma((SLOTS,)),
            dma((SLOTS,)),
            dma((7,)),
            dma((7,)),
        ]
        + wave_scratch(96)
        + wave_scratch(96)
        + wave_scratch(32),
        compiler_params=pltpu.CompilerParams(
            collective_id=1, has_side_effects=True, vmem_limit_bytes=VMEM_LIMIT
        ),
        name="sums",
    )(*operands)


def last_kernel(
    edge_factor, node_factor, sums_ref, part_ref, npart_ref, grad_ref, ein_ref, eout_ref, nin_ref, nout_ref
):
    grad_ref[...] = npart_ref[...] + part_ref[...].astype(F32)
    nin_ref[0] = sums_ref[0:8, :] * node_factor
    nout_ref[0] = sums_ref[8:12, :] * node_factor
    ein_ref[...] = (sums_ref[12:24, :] * edge_factor).reshape(12, 1, L)
    eout_ref[0] = sums_ref[24:28, :] * edge_factor


def run_last(edge_factor, node_factor, *operands):
    vmem = pl.BlockSpec(memory_space=pltpu.VMEM)
    shape = jax.ShapeDtypeStruct
    return pl.pallas_call(
        functools.partial(last_kernel, edge_factor, node_factor),
        out_shape=[
            shape((N, L), F32),
            shape((12, 1, L), F32),
            shape((1, 4, L), F32),
            shape((1, 8, L), F32),
            shape((1, 4, L), F32),
        ],
        in_specs=[vmem] * 3,
        out_specs=[vmem] * 5,
        name="last",
    )(*operands)


def per_device(
    node_latent,
    edge_latent,
    sender_index,
    receiver_index,
    send_rows,
    node_count,
    edge_proj_in,
    edge_bias_in,
    edge_proj_out,
    edge_bias_out,
    edge_gain,
    node_proj_in,
    node_bias_in,
    node_proj_out,
    node_bias_out,
    node_gain,
    node_cot,
    edge_cot,
):
    n_dom = lax.axis_size("dom")
    slot_rows = send_rows.transpose(0, 2, 1).reshape(HB, n_dom)
    snd = sender_index.reshape(E // 128, 128)
    rcv = receiver_index.reshape(E // 128, 128)
    pin, pout = edge_proj_in.reshape(3 * L, L), edge_proj_out.reshape(L, L)
    halo, thalo, pre_part = run_halo(
        n_dom, snd, rcv, slot_rows, node_latent, edge_latent, pin, edge_bias_in
    )
    node_out, edge_out, edge_grad, dpre, draw, hid, gnode, npart = run_rows(
        n_dom, snd, rcv, node_count, thalo, node_latent, pre_part, edge_latent, pin, pout,
        edge_bias_out, edge_gain, node_proj_in.reshape(2 * L, L), node_bias_in,
        node_proj_out.reshape(L, L), node_bias_out, node_gain, node_cot, edge_cot,
    )
    sums, part = run_sums(
        n_dom, snd, rcv, slot_rows, gnode, node_latent, halo, edge_latent, pin, hid, draw, dpre
    )
    edge_factor = float(E * n_dom) ** (-0.5)
    node_factor = float(N * n_dom) ** (-0.5)
    node_grad, edge_in, edge_out_grad, node_in, node_out_grad = run_last(
        edge_factor, node_factor, sums, part, npart
    )
    edge_in = edge_in.transpose(1, 0, 2)
    return node_out, edge_out, node_grad, edge_grad, edge_in, edge_out_grad, node_in, node_out_grad


def solution(mesh):
    rows = P("dom", None)
    one = P("dom")
    whole = P()
    in_specs = (rows, rows, one, one, P("dom", None, None), one) + (whole,) * 10 + (rows, rows)
    split = P(None, "dom", None)
    out_specs = (rows,) * 4 + (split,) * 4
    return jax.shard_map(per_device, mesh=mesh, in_specs=in_specs, out_specs=out_specs, check_vma=False)
```

```python
import functools

import jax
import jax.numpy as jnp
from jax import lax
from jax.experimental import pallas as pl
from jax.experimental.pallas import tpu as pltpu
from jax.sharding import PartitionSpec as P

EPS = 1e-05
MESH = pl.DeviceIdType.MESH
BF = jnp.bfloat16
F32 = jnp.float32
I32 = jnp.int32

L = 512
N = 512
E = 2048
HB = 8
SLOTS = 9
HALO = SLOTS * HB
HPAD = 128
TAB = N + HPAD
C = 512
CHUNKS = E // C
S = 256
WIDE = L // 2
LANES = 128
VMEM_LIMIT = 56 * 1024 * 1024

NT = (((1,), (1,)), ((), ()))
TN = (((0,), (0,)), ((), ()))


def slot_shift(slot):
    return 64 if slot == 4 else slot - 4


def mm(a, b):
    return jnp.dot(a, b, preferred_element_type=F32)


def mm_nt(a, b):
    return lax.dot_general(a, b, NT, preferred_element_type=F32)


def mm_tn(a, b):
    return lax.dot_general(a, b, TN, preferred_element_type=F32)


def staggered(*streams):
    live = list(streams)
    turn = 0
    while live:
        for stream in live[: turn + 1]:
            if next(stream, StopIteration) is StopIteration:
                live.remove(stream)
                turn -= 1
        turn += 1


def sigmoid(x):
    return 0.5 * jnp.tanh(0.5 * x) + 0.5


def table_index(sender, me, n_dom):
    far = sender - N
    peer = far // HB
    row = far - peer * HB
    turn = lax.rem(peer - me + (n_dom + 4), n_dom)
    slot = jnp.where(turn == 68, 4, turn)
    return jnp.where(sender < N, sender, N + slot * HB + row)


def boundary_rows(rows_ref, readers):
    lane = lax.broadcasted_iota(I32, (HB, 128), 1)
    node = lax.broadcasted_iota(I32, (HB, N), 1)
    listed = rows_ref[...]
    picked = []
    for reader in readers:
        column = jnp.sum(jnp.where(lane == reader, listed, 0), axis=1, keepdims=True)
        picked.append((jnp.broadcast_to(column, (HB, N)) == node).astype(F32))
    return jnp.concatenate(picked, axis=0).astype(BF)


def greet(devices):
    barrier = pltpu.get_barrier_semaphore()
    for device in devices:
        pl.semaphore_signal(barrier, inc=1, device_id=(device,), device_id_type=MESH)
    pl.semaphore_wait(barrier, len(devices))


def one_hot_columns(index, lane, blocks):
    column = jnp.broadcast_to(index, (128, 128)).T
    return jnp.concatenate(
        [(column == lane + 128 * m).astype(F32).astype(BF) for m in range(blocks)], axis=1
    )


def halo_kernel(
    n_dom,
    snd_ref, rcv_ref, rows_ref, h_hbm, e_hbm, pin_hbm, b_in,
    halo_ref, thalo_ref, pre_hbm,
    h_v, x_v, pin_v, t_v, pre_v, outgoing, incoming,
    in_sem, e_sem, pre_sem, send_sem, recv_sem,
):
    me = lax.axis_index("dom")
    targets = [lax.rem(me - slot_shift(s) + n_dom, n_dom) for s in range(SLOTS)]

    def rows(i):
        return pl.ds(pl.multiple_of(i * C, C), C)

    def e_load(i):
        return pltpu.make_async_copy(e_hbm.at[rows(i)], x_v.at[rows(i), pl.ds(0, L)], e_sem.at[i])

    def pre_put(i):
        return pltpu.make_async_copy(pre_v.at[rows(i)], pre_hbm.at[rows(i)], pre_sem.at[i])

    barrier = pltpu.get_barrier_semaphore()
    for device in targets:
        pl.semaphore_signal(barrier, inc=1, device_id=(device,), device_id_type=MESH)
    h_load = pltpu.make_async_copy(h_hbm, h_v, in_sem.at[0])
    h_load.start()
    pin_load = pltpu.make_async_copy(pin_hbm, pin_v, in_sem.at[1])
    pin_load.start()
    for i in range(CHUNKS):
        e_load(i).start()
    h_load.wait()
    outgoing[...] = mm(boundary_rows(rows_ref, targets), h_v[...])
    pl.semaphore_wait(barrier, SLOTS)
    copies = []
    for s in range(SLOTS):
        copy = pltpu.make_async_remote_copy(
            src_ref=outgoing.at[pl.ds(s * HB, HB)],
            dst_ref=incoming.at[pl.ds(s * HB, HB)],
            send_sem=send_sem.at[s],
            recv_sem=recv_sem.at[s],
            device_id=(targets[s],),
            device_id_type=MESH,
        )
        copy.start()
        copies.append(copy)

    pin_load.wait()
    t_v[0:L, :] = pin_v[0:L, :]
    t_v[L : 2 * L, :] = mm(h_v[...], pin_v[L : 2 * L, :]).astype(BF)
    t_v[2 * L :, :] = (mm(h_v[...], pin_v[2 * L :, :]) + b_in[...]).astype(BF)
    lane = lax.broadcasted_iota(I32, (128, 128), 1)

    def local(first):
        if first % C == 0:
            e_load(first // C).wait()
        for b in range(S // 128):
            at = pl.ds(first + b * 128, 128)
            block = pl.ds(first // 128 + b, 1)
            x_v[at, L : 2 * L] = one_hot_columns(snd_ref[block, :], lane, N // 128)
            x_v[at, 2 * L :] = one_hot_columns(rcv_ref[block, :], lane, N // 128)
        yield
        at = pl.ds(first, S)
        pre_v[at, :] = mm(x_v[at, :], t_v[...]).astype(BF)
        if (first + S) % C == 0:
            pre_put(first // C).start()

    staggered(*[local(s * S) for s in range(E // S)])
    for copy in copies:
        copy.wait()
    halo = jnp.concatenate([incoming[...].astype(BF), jnp.zeros((HPAD - HALO, L), BF)], axis=0)
    halo_ref[...] = halo
    thalo_ref[...] = mm(halo, pin_v[L : 2 * L, :]).astype(BF)
    for i in range(CHUNKS):
        pre_put(i).wait()


def run_halo(n_dom, *operands):
    hbm = pl.BlockSpec(memory_space=pl.ANY)
    vmem = pl.BlockSpec(memory_space=pltpu.VMEM)
    shape = jax.ShapeDtypeStruct
    dma = pltpu.SemaphoreType.DMA
    return pl.pallas_call(
        functools.partial(halo_kernel, n_dom),
        out_shape=[shape((HPAD, L), BF), shape((HPAD, L), BF), shape((E, L), BF)],
        in_specs=[vmem, vmem, vmem, hbm, hbm, hbm, vmem],
        out_specs=[vmem, vmem, hbm],
        scratch_shapes=[
            pltpu.VMEM((N, L), BF),
            pltpu.VMEM((E, 3 * L), BF),
            pltpu.VMEM((3 * L, L), BF),
            pltpu.VMEM((3 * L, L), BF),
            pltpu.VMEM((E, L), BF),
            pltpu.VMEM((HALO, L), F32),
            pltpu.VMEM((HALO, L), F32),
            dma((2,)),
            dma((CHUNKS,)),
            dma((CHUNKS,)),
            dma((SLOTS,)),
            dma((SLOTS,)),
        ],
        compiler_params=pltpu.CompilerParams(
            collective_id=0, has_side_effects=True, vmem_limit_bytes=VMEM_LIMIT
        ),
        name="halo",
    )(*operands)


def norm_forward(raw):
    centered = raw - jnp.mean(raw, axis=-1, keepdims=True)
    inv = lax.rsqrt(jnp.mean(centered * centered, axis=-1, keepdims=True) + EPS)
    return centered * inv, inv


def norm_backward(q, normed, inv):
    first = jnp.mean(q, axis=-1, keepdims=True)
    second = jnp.mean(q * normed, axis=-1, keepdims=True)
    return inv * (q - first - normed * second)


def act_slope(pre):
    gate = sigmoid(pre)
    return gate * (1.0 + pre * (1.0 - gate))


def rows_kernel(
    n_dom,
    snd_ref, rcv_ref, cnt_ref, thalo_ref, h_hbm, part_hbm, e_hbm, pin_hbm, pout_hbm, b_out, gain,
    npin_hbm, nb_in, npout_hbm, nb_out, ngain, ncot_hbm, ecot_hbm,
    nout_hbm, eout_hbm, egrad_hbm, dpre_hbm, draw_hbm, hid_hbm, gnode_hbm, npart_hbm,
    idx_v, x_v, rt_v, e_v, part_v, h_v, pe_v, pout_v, npin_v, npout_v, ncot_v, cot_v,
    slope_v, hid_v, n_v, inv_v, enew_v, draw_v, dpre_v, nx_v, dy_v, nout_v, npart_v, gnode_v,
    in_sem, e_sem, part_sem, cot_sem, eout_sem, hid_sem, draw_sem, dpre_sem, egrad_sem, out_sem,
):
    me = lax.axis_index("dom")

    def load(k, src, dst):
        return pltpu.make_async_copy(src, dst, in_sem.at[k])

    def rows(i):
        return pl.ds(pl.multiple_of(i * C, C), C)

    def e_load(i):
        return pltpu.make_async_copy(e_hbm.at[rows(i)], e_v.at[rows(i)], e_sem.at[i])

    def part_load(i):
        return pltpu.make_async_copy(part_hbm.at[rows(i)], part_v.at[rows(i)], part_sem.at[i])

    def cot_load(i):
        return pltpu.make_async_copy(ecot_hbm.at[rows(i)], cot_v.at[rows(i)], cot_sem.at[i])

    def put(i, src, dst, sem):
        return pltpu.make_async_copy(src.at[rows(i)], dst.at[rows(i)], sem.at[i])

    loads = [
        load(0, pout_hbm, pout_v),
        load(1, h_hbm, h_v),
        load(2, npin_hbm, npin_v),
        load(3, npout_hbm, npout_v),
        load(4, ncot_hbm, ncot_v),
        load(5, pin_hbm.at[pl.ds(0, L)], pe_v),
    ]
    part_load(0).start()
    loads[0].start()
    for i in range(CHUNKS):
        e_load(i).start()
        if i + 1 < CHUNKS:
            part_load(i + 1).start()
    for k in range(1, 6):
        loads[k].start()
    for i in range(CHUNKS):
        cot_load(i).start()

    idx_v[...] = table_index(snd_ref[...], me, n_dom)
    lane = lax.broadcasted_iota(I32, (128, 128), 1)
    high = lax.broadcasted_iota(I32, (N, 128), 0)
    loads[0].wait()

    def forward_rows(first):
        if first % C == 0:
            part_load(first // C).wait()
            e_load(first // C).wait()
        for b in range(S // 128):
            at = pl.ds(pl.multiple_of(first + b * 128, 128), 128)
            block = first // 128 + b
            r_row = rcv_ref[pl.ds(block, 1), :]
            x_v[at, 0:HPAD] = one_hot_columns(idx_v[pl.ds(block, 1), :] - N, lane, 1)
            x_v[at, HPAD:] = one_hot_columns(r_row, lane, N // 128)
            rt_v[:, at] = (jnp.broadcast_to(r_row, (N, 128)) == high).astype(F32).astype(BF)
        at = pl.ds(pl.multiple_of(first, S), S)
        pre = part_v[at, :].astype(F32) + mm(x_v[at, 0:HPAD], thalo_ref[...])
        yield
        gate = sigmoid(pre)
        hidden = pre * gate
        slope_v[at, :] = (gate + hidden * (1.0 - gate)).astype(BF)
        hid = hidden.astype(BF)
        hid_v[at, :] = hid
        yield
        raw = mm(hid, pout_v[...]) + b_out[...]
        yield
        normed, inv = norm_forward(raw)
        n_v[at, :] = normed
        inv_v[at, :] = inv
        enew_v[at, :] = (e_v[at, :].astype(F32) + normed * gain[...]).astype(BF)
        if (first + S) % C == 0:
            put(first // C, enew_v, eout_hbm, eout_sem).start()
            put(first // C, hid_v, hid_hbm, hid_sem).start()

    staggered(*[forward_rows(s * S) for s in range(E // S)])

    valid = (lax.broadcasted_iota(I32, (N, 1), 0) < cnt_ref[0]).astype(F32)
    nx_v[:, L:] = (mm(rt_v[...], enew_v[...]) * valid).astype(BF)
    for k in range(1, 6):
        loads[k].wait()
    nx_v[:, 0:L] = h_v[...]
    pre = mm(nx_v[...], npin_v[...]) + nb_in[...]
    hid = (pre * sigmoid(pre)).astype(BF)
    normed, inv = norm_forward(mm(hid, npout_v[...]) + nb_out[...])
    nout_v[...] = (h_v[...].astype(F32) + valid * (normed * ngain[...])).astype(BF)
    nout_copy = pltpu.make_async_copy(nout_v, nout_hbm, out_sem.at[0])
    nout_copy.start()
    draw = norm_backward(valid * ncot_v[...] * ngain[...], normed, inv).astype(BF)
    dpre = (mm_nt(draw, npout_v[...]) * act_slope(pre)).astype(BF)
    npart_v[...] = ncot_v[...] + mm_nt(dpre, npin_v[0:L, :])
    npart_copy = pltpu.make_async_copy(npart_v, npart_hbm, out_sem.at[1])
    npart_copy.start()
    dy_v[...] = mm_nt(dpre, npin_v[L:, :]).astype(BF)
    grad_in = mm_tn(nx_v[...], dpre).astype(BF)
    grad_out = mm_tn(hid, draw).astype(BF)
    for k in range(4):
        columns = slice(LANES * k, LANES * (k + 1))
        gnode_v[k, :, 0:64, :] = grad_in[:, columns].reshape(16, 64, LANES)
        gnode_v[k, :, 64:96, :] = grad_out[:, columns].reshape(16, 32, LANES)
    gnode_copy = pltpu.make_async_copy(gnode_v, gnode_hbm, out_sem.at[2])
    gnode_copy.start()

    def backward_rows(first):
        if first % C == 0:
            cot_load(first // C).wait()
        at = pl.ds(pl.multiple_of(first, S), S)
        total = cot_v[at, :] + mm(x_v[at, HPAD:], dy_v[...])
        yield
        draw = norm_backward(total * gain[...], n_v[at, :], inv_v[at, :]).astype(BF)
        draw_v[at, :] = draw
        yield
        dhid = mm_nt(draw, pout_v[...])
        yield
        dpre = (dhid * slope_v[at, :].astype(F32)).astype(BF)
        dpre_v[at, :] = dpre
        yield
        cot_v[at, :] = total + mm_nt(dpre, pe_v[...])
        if (first + S) % C == 0:
            put(first // C, draw_v, draw_hbm, draw_sem).start()
            put(first // C, dpre_v, dpre_hbm, dpre_sem).start()
            put(first // C, cot_v, egrad_hbm, egrad_sem).start()

    staggered(*[backward_rows(s * S) for s in range(E // S)])
    nout_copy.wait()
    npart_copy.wait()
    gnode_copy.wait()
    for i in range(CHUNKS):
        put(i, enew_v, eout_hbm, eout_sem).wait()
        put(i, hid_v, hid_hbm, hid_sem).wait()
        put(i, draw_v, draw_hbm, draw_sem).wait()
        put(i, dpre_v, dpre_hbm, dpre_sem).wait()
        put(i, cot_v, egrad_hbm, egrad_sem).wait()


def run_rows(n_dom, *operands):
    hbm = pl.BlockSpec(memory_space=pl.ANY)
    vmem = pl.BlockSpec(memory_space=pltpu.VMEM)
    smem = pl.BlockSpec(memory_space=pltpu.SMEM)
    shape = jax.ShapeDtypeStruct
    dma = pltpu.SemaphoreType.DMA
    return pl.pallas_call(
        functools.partial(rows_kernel, n_dom),
        out_shape=[
            shape((N, L), BF),
            shape((E, L), BF),
            shape((E, L), F32),
            shape((E, L), BF),
            shape((E, L), BF),
            shape((E, L), BF),
            shape((4, 16, 96, LANES), BF),
            shape((N, L), F32),
        ],
        in_specs=[vmem, vmem, smem, vmem, hbm, hbm, hbm, hbm, hbm, vmem, vmem]
        + [hbm, vmem, hbm, vmem, vmem, hbm, hbm],
        out_specs=[hbm] * 8,
        scratch_shapes=[
            pltpu.VMEM((16, 128), I32),
            pltpu.VMEM((E, HPAD + N), BF),
            pltpu.VMEM((N, E), BF),
            pltpu.VMEM((E, L), BF),
            pltpu.VMEM((E, L), BF),
            pltpu.VMEM((N, L), BF),
            pltpu.VMEM((L, L), BF),
            pltpu.VMEM((L, L), BF),
            pltpu.VMEM((2 * L, L), BF),
            pltpu.VMEM((L, L), BF),
            pltpu.VMEM((N, L), F32),
            pltpu.VMEM((E, L), F32),
            pltpu.VMEM((E, L), BF),
            pltpu.VMEM((E, L), BF),
            pltpu.VMEM((E, L), F32),
            pltpu.VMEM((E, 1), F32),
            pltpu.VMEM((E, L), BF),
            pltpu.VMEM((E, L), BF),
            pltpu.VMEM((E, L), BF),
            pltpu.VMEM((N, 2 * L), BF),
            pltpu.VMEM((N, L), BF),
            pltpu.VMEM((N, L), BF),
            pltpu.VMEM((N, L), F32),
            pltpu.VMEM((4, 16, 96, LANES), BF),
            dma((6,)),
            dma((CHUNKS,)),
            dma((CHUNKS,)),
            dma((CHUNKS,)),
            dma((CHUNKS,)),
            dma((CHUNKS,)),
            dma((CHUNKS,)),
            dma((CHUNKS,)),
            dma((CHUNKS,)),
            dma((3,)),
        ],
        compiler_params=pltpu.CompilerParams(vmem_limit_bytes=VMEM_LIMIT),
        name="rows",
    )(*operands)


class Wave:
    def __init__(self, coords, refs):
        self.coords = coords
        (self.own, self.from_core, self.a1, self.b1, self.sa, self.sb, self.a2, self.b2) = refs[:8]
        self.send, self.recv = refs[8:]
        self.copies = []

    def start(self, src, dst, device):
        k = len(self.copies)
        copy = pltpu.make_async_remote_copy(
            src_ref=src,
            dst_ref=dst,
            send_sem=self.send.at[k],
            recv_sem=self.recv.at[k],
            device_id=(device,),
            device_id_type=MESH,
        )
        copy.start()
        self.copies.append(copy)

    def to_core(self, src, into=None):
        z, x, y, c = self.coords
        self.start(src, self.from_core if into is None else into, device_at(z, x, y, 1 - c))

    def first(self):
        z, x, y, c = self.coords
        self.copies[0].wait_recv()
        own, got = self.own, self.from_core
        for zz in range(4):
            own[0, zz] = (own[0, zz].astype(F32) + got[0, zz].astype(F32)).astype(BF)
        for o in (2, 1, 3):
            zp = lax.rem(z + 4 - o, 4)
            self.start(own.at[0, zp], self.a1.at[o - 1], device_at(zp, x, y, c))
        for zz in range(4):
            own[1, zz] = (own[1, zz].astype(F32) + got[1, zz].astype(F32)).astype(BF)
        for o in (2, 1, 3):
            xp = lax.rem(x + 4 - o, 4)
            self.start(own.at[1, :, xp], self.b1.at[o - 1], device_at(z, xp, y, c))

    def second(self):
        z, x, y, c = self.coords
        for copy in self.copies[1:4]:
            copy.wait_recv()
        a = self.own[0, z].astype(F32)
        for o in range(3):
            a = a + self.a1[o].astype(F32)
        self.sa[...] = a.astype(BF)
        for o in (2, 1, 3):
            xp = lax.rem(x + 4 - o, 4)
            self.start(self.sa.at[xp], self.a2.at[o - 1], device_at(z, xp, y, c))
        for copy in self.copies[4:7]:
            copy.wait_recv()
        b = self.own[1, :, x].astype(F32)
        for o in range(3):
            b = b + self.b1[o].astype(F32)
        self.sb[...] = b.astype(BF)
        for o in (2, 1, 3):
            zp = lax.rem(z + 4 - o, 4)
            self.start(self.sb.at[zp], self.b2.at[o - 1], device_at(zp, x, y, c))

    def third(self, block, at):
        z, x, y, c = self.coords
        for copy in self.copies[7:13]:
            copy.wait_recv()
        a, b = self.sa[x].astype(F32), self.sb[z].astype(F32)
        for o in range(3):
            a = a + self.a2[o].astype(F32)
            b = b + self.b2[o].astype(F32)
        block[at, 0:LANES] = a.astype(BF)
        block[at, LANES:WIDE] = b.astype(BF)

    def finish(self):
        for copy in self.copies:
            copy.wait_send()


def device_at(z, x, y, c):
    return ((z * 4 + x) * 4 + y) * 2 + c


def wave_scratch(depth):
    dma = pltpu.SemaphoreType.DMA
    return [
        pltpu.VMEM((2, 4, 4, depth, LANES), BF),
        pltpu.VMEM((2, 4, 4, depth, LANES), BF),
        pltpu.VMEM((3, 4, depth, LANES), BF),
        pltpu.VMEM((3, 4, depth, LANES), BF),
        pltpu.VMEM((4, depth, LANES), BF),
        pltpu.VMEM((4, depth, LANES), BF),
        pltpu.VMEM((3, depth, LANES), BF),
        pltpu.VMEM((3, depth, LANES), BF),
        dma((13,)),
        dma((13,)),
    ]


def sums_kernel(
    n_dom,
    snd_ref, rcv_ref, rows_ref, gnode_hbm, h_hbm, halo_hbm, e_hbm, pin_hbm, hid_hbm, draw_hbm, dpre_hbm,
    out_ref, part_ref,
    tab_v, e_v, hid_v, draw_v, dpre_v, ps_v, pr_v, st_v, rt_v, as_v, ar_v, there_in, there_out, y_v, ret_ref, part_v,
    block, sorted_v, got, in_sem, y_send, y_recv, last_send, last_recv,
    *wave_refs,
):
    me = lax.axis_index("dom")
    c = lax.rem(me, 2)
    y = lax.rem(me // 2, 4)
    x = lax.rem(me // 8, 4)
    z = me // 32
    m = lax.rem(me, 8)
    coords = (z, x, y, c)
    node_wave = Wave(coords, wave_refs[0:10])
    in_wave = Wave(coords, wave_refs[10:20])
    out_wave = Wave(coords, wave_refs[20:30])

    mine = pl.ds(pl.multiple_of(c * WIDE, WIDE), WIDE)
    theirs = pl.ds(pl.multiple_of((1 - c) * WIDE, WIDE), WIDE)
    halves = (theirs, mine)

    loads = []

    def load(src, dst):
        copy = pltpu.make_async_copy(src, dst, in_sem.at[len(loads)])
        copy.start()
        loads.append(copy)

    for lanes in range(2):
        for k in range(4):
            load(gnode_hbm.at[2 * c + lanes, pl.ds(4 * k, 4)], node_wave.own.at[lanes, k])
    load(dpre_hbm.at[:, theirs], dpre_v.at[0])
    load(e_hbm, e_v)
    load(h_hbm, tab_v.at[pl.ds(0, N)])
    load(halo_hbm, tab_v.at[pl.ds(N, HPAD)])
    load(dpre_hbm.at[:, mine], dpre_v.at[1])
    load(hid_hbm, hid_v)
    load(draw_hbm.at[:, theirs], draw_v.at[0])
    load(draw_hbm.at[:, mine], draw_v.at[1])
    for half in range(2):
        load(pin_hbm.at[pl.ds(L, L), halves[half]], ps_v.at[half])
        load(pin_hbm.at[pl.ds(2 * L, L), halves[half]], pr_v.at[half])

    owners = [lax.rem(me + slot_shift(s) + n_dom, n_dom) for s in range(SLOTS)]
    others = [device_at(z, x, 0, 0) + lax.rem(m + 8 - o, 8) for o in range(1, 8)]
    along = [device_at(lax.rem(z + o, 4), x, y, c) for o in range(1, 4)]
    along += [device_at(z, lax.rem(x + o, 4), y, c) for o in range(1, 4)]
    greet(owners + others + along)

    node_wave.to_core(gnode_hbm.at[pl.ds(2 * (1 - c), 2)], node_wave.from_core.reshape(2, 16, 96, LANES))

    index = table_index(snd_ref[...], me, n_dom)
    high = lax.broadcasted_iota(I32, (TAB, 128), 0)
    for k in range(E // 128):
        at = pl.ds(k * 128, 128)
        st_v[:, at] = (jnp.broadcast_to(index[k : k + 1, :], (TAB, 128)) == high).astype(F32).astype(BF)
        rt_v[:, at] = (
            (jnp.broadcast_to(rcv_ref[k : k + 1, :], (N, 128)) == high[0:N, :]).astype(F32).astype(BF)
        )

    def put_lanes(product, dst, depth):
        for lanes in range(2):
            part = product[:, LANES * lanes : LANES * (lanes + 1)]
            dst[lanes] = part.astype(BF).reshape(4, 4, depth, LANES)

    def in_products(half, dst):
        dpre = dpre_v[half]
        sent = mm(st_v[...], dpre).astype(BF)
        taken = mm(rt_v[...], dpre).astype(BF)
        as_v[half] = sent
        ar_v[half] = taken
        product = jnp.concatenate(
            [mm_tn(e_v[...], dpre), mm_tn(tab_v[...], sent), mm_tn(tab_v[0:N, :], taken)], axis=0
        )
        put_lanes(product, dst, 96)

    def out_products(half, dst):
        put_lanes(mm_tn(hid_v[...], draw_v[half]), dst, 32)

    for k in range(8):
        loads[k].wait()
    node_wave.first()
    for k in range(8, 12):
        loads[k].wait()
    in_products(0, there_in)
    in_wave.to_core(there_in)
    loads[12].wait()
    in_products(1, in_wave.own)
    in_wave.first()
    for k in range(13, 20):
        loads[k].wait()
    out_products(0, there_out)
    out_wave.to_core(there_out)
    node_wave.second()
    out_products(1, out_wave.own)
    out_wave.first()

    y_v[...] = mm_nt(as_v[0, N : N + HALO, :], ps_v[0]) + mm_nt(as_v[1, N : N + HALO, :], ps_v[1])
    returns = []
    for s in range(SLOTS):
        copy = pltpu.make_async_remote_copy(
            src_ref=y_v.at[pl.ds(s * HB, HB)],
            dst_ref=ret_ref.at[pl.ds(s * HB, HB)],
            send_sem=y_send.at[s],
            recv_sem=y_recv.at[s],
            device_id=(owners[s],),
            device_id_type=MESH,
        )
        copy.start()
        returns.append(copy)
    in_wave.second()
    out_wave.second()
    part_v[...] = (
        mm_nt(as_v[0, 0:N, :], ps_v[0])
        + mm_nt(as_v[1, 0:N, :], ps_v[1])
        + mm_nt(ar_v[0], pr_v[0])
        + mm_nt(ar_v[1], pr_v[1])
    )
    node_wave.third(block, pl.ds(0, 96))
    row = lax.broadcasted_iota(I32, (256, 224), 0)
    col = lax.broadcasted_iota(I32, (256, 224), 1)
    j = row // 32
    r = row - j * 32
    source = jnp.where(
        r < 8,
        8 * j + r,
        jnp.where(
            r < 12,
            64 + 4 * j + (r - 8),
            jnp.where(r < 24, 96 + 12 * j + (r - 12), jnp.where(r < 28, 192 + 4 * j + (r - 24), -1)),
        ),
    )
    order = (source == col).astype(F32).astype(BF)
    for copy in returns:
        copy.wait()
    readers = [lax.rem(me - slot_shift(s) + n_dom, n_dom) for s in range(SLOTS)]
    part_ref[...] = (part_v[...] + mm_tn(boundary_rows(rows_ref, readers), ret_ref[...].astype(BF))).astype(BF)
    in_wave.third(block, pl.ds(96, 96))
    out_wave.third(block, pl.ds(192, 32))

    sorted_v[...] = mm(order, block[...]).astype(BF).reshape(8, 32, WIDE)
    lasts = []
    for o in range(1, 8):
        target = lax.rem(m + 8 - o, 8)
        copy = pltpu.make_async_remote_copy(
            src_ref=sorted_v.at[target],
            dst_ref=got.at[o - 1],
            send_sem=last_send.at[o - 1],
            recv_sem=last_recv.at[o - 1],
            device_id=(others[o - 1],),
            device_id_type=MESH,
        )
        copy.start()
        lasts.append(copy)
    for copy in lasts:
        copy.wait_recv()
    same = sorted_v[m].astype(F32)
    for o in (2, 4, 6):
        same = same + got[o - 1].astype(F32)
    cross = got[0].astype(F32)
    for o in (3, 5, 7):
        cross = cross + got[o - 1].astype(F32)
    even = c == 0
    out_ref[:, 0:WIDE] = jnp.where(even, same, cross)
    out_ref[:, WIDE:] = jnp.where(even, cross, same)
    for copy in lasts:
        copy.wait_send()
    for wave in (node_wave, in_wave, out_wave):
        wave.finish()


def run_sums(n_dom, *operands):
    hbm = pl.BlockSpec(memory_space=pl.ANY)
    vmem = pl.BlockSpec(memory_space=pltpu.VMEM)
    shape = jax.ShapeDtypeStruct
    dma = pltpu.SemaphoreType.DMA
    return pl.pallas_call(
        functools.partial(sums_kernel, n_dom),
        out_shape=[shape((32, L), F32), shape((N, L), BF)],
        in_specs=[vmem, vmem, vmem] + [hbm] * 8,
        out_specs=[vmem, vmem],
        scratch_shapes=[
            pltpu.VMEM((TAB, L), BF),
            pltpu.VMEM((E, L), BF),
            pltpu.VMEM((E, L), BF),
            pltpu.VMEM((2, E, WIDE), BF),
            pltpu.VMEM((2, E, WIDE), BF),
            pltpu.VMEM((2, L, WIDE), BF),
            pltpu.VMEM((2, L, WIDE), BF),
            pltpu.VMEM((TAB, E), BF),
            pltpu.VMEM((N, E), BF),
            pltpu.VMEM((2, TAB, WIDE), BF),
            pltpu.VMEM((2, N, WIDE), BF),
            pltpu.VMEM((2, 4, 4, 96, LANES), BF),
            pltpu.VMEM((2, 4, 4, 32, LANES), BF),
            pltpu.VMEM((HALO, L), F32),
            pltpu.VMEM((HALO, L), F32),
            pltpu.VMEM((N, L), F32),
            pltpu.VMEM((224, WIDE), BF),
            pltpu.VMEM((8, 32, WIDE), BF),
            pltpu.VMEM((7, 32, WIDE), BF),
            dma((20,)),
            dma((SLOTS,)),
            dma((SLOTS,)),
            dma((7,)),
            dma((7,)),
        ]
        + wave_scratch(96)
        + wave_scratch(96)
        + wave_scratch(32),
        compiler_params=pltpu.CompilerParams(
            collective_id=1, has_side_effects=True, vmem_limit_bytes=VMEM_LIMIT
        ),
        name="sums",
    )(*operands)


def last_kernel(
    edge_factor, node_factor, sums_ref, part_ref, npart_ref, grad_ref, ein_ref, eout_ref, nin_ref, nout_ref
):
    grad_ref[...] = npart_ref[...] + part_ref[...].astype(F32)
    nin_ref[0] = sums_ref[0:8, :] * node_factor
    nout_ref[0] = sums_ref[8:12, :] * node_factor
    ein_ref[...] = (sums_ref[12:24, :] * edge_factor).reshape(12, 1, L)
    eout_ref[0] = sums_ref[24:28, :] * edge_factor


def run_last(edge_factor, node_factor, *operands):
    vmem = pl.BlockSpec(memory_space=pltpu.VMEM)
    shape = jax.ShapeDtypeStruct
    return pl.pallas_call(
        functools.partial(last_kernel, edge_factor, node_factor),
        out_shape=[
            shape((N, L), F32),
            shape((12, 1, L), F32),
            shape((1, 4, L), F32),
            shape((1, 8, L), F32),
            shape((1, 4, L), F32),
        ],
        in_specs=[vmem] * 3,
        out_specs=[vmem] * 5,
        name="last",
    )(*operands)


def per_device(
    node_latent,
    edge_latent,
    sender_index,
    receiver_index,
    send_rows,
    node_count,
    edge_proj_in,
    edge_bias_in,
    edge_proj_out,
    edge_bias_out,
    edge_gain,
    node_proj_in,
    node_bias_in,
    node_proj_out,
    node_bias_out,
    node_gain,
    node_cot,
    edge_cot,
):
    n_dom = lax.axis_size("dom")
    slot_rows = send_rows.transpose(0, 2, 1).reshape(HB, n_dom)
    snd = sender_index.reshape(E // 128, 128)
    rcv = receiver_index.reshape(E // 128, 128)
    pin, pout = edge_proj_in.reshape(3 * L, L), edge_proj_out.reshape(L, L)
    halo, thalo, pre_part = run_halo(
        n_dom, snd, rcv, slot_rows, node_latent, edge_latent, pin, edge_bias_in
    )
    node_out, edge_out, edge_grad, dpre, draw, hid, gnode, npart = run_rows(
        n_dom, snd, rcv, node_count, thalo, node_latent, pre_part, edge_latent, pin, pout,
        edge_bias_out, edge_gain, node_proj_in.reshape(2 * L, L), node_bias_in,
        node_proj_out.reshape(L, L), node_bias_out, node_gain, node_cot, edge_cot,
    )
    sums, part = run_sums(
        n_dom, snd, rcv, slot_rows, gnode, node_latent, halo, edge_latent, pin, hid, draw, dpre
    )
    edge_factor = float(E * n_dom) ** (-0.5)
    node_factor = float(N * n_dom) ** (-0.5)
    node_grad, edge_in, edge_out_grad, node_in, node_out_grad = run_last(
        edge_factor, node_factor, sums, part, npart
    )
    edge_in = edge_in.transpose(1, 0, 2)
    return node_out, edge_out, node_grad, edge_grad, edge_in, edge_out_grad, node_in, node_out_grad


def solution(mesh):
    rows = P("dom", None)
    one = P("dom")
    whole = P()
    in_specs = (rows, rows, one, one, P("dom", None, None), one) + (whole,) * 10 + (rows, rows)
    split = P(None, "dom", None)
    out_specs = (rows,) * 4 + (split,) * 4
    return jax.shard_map(per_device, mesh=mesh, in_specs=in_specs, out_specs=out_specs, check_vma=False)
```
